32 devices in a mesh: grp: 4 (over z), wide: 8 (over y, x, core).
Axes of the slice: x: 2, y: 2, z: 4, core: 2. Of those that a mesh axis runs over, the one named last changes fastest.
Arguments:
- half_integrals: bfloat16 [8, 4, 1024, 2048], P('wide', None, None, 'grp'), may hold values from -0.47851562 to 0.47851562
- coeff_virtual: bfloat16 [1024, 768], replicated, may hold values from -0.1875 to 0.1875
- occ_energy: float32 [8, 4], replicated, may hold values from -2 to -0.3
- vir_energy: float32 [768], replicated, may hold values from 0.2 to 3
- plan: int32 [2, 2], replicated, may hold values from 0 to 7, as said below
Outputs:
- density_three: float32 [8, 4, 768, 2048], P('wide', 'grp')
The draws below stay inside these ranges and needn't reach their ends.
Inputs may be any that keep to these rules, and one draw needn't show every extreme that they name: plan[s, k] is the owner block whose orbitals serve step s, slot k; the value 0 and the value 8 - 1 both occur in every draw, an owner may repeat.
All inputs are finite; a program needn't handle non-finite values.
Results may differ from the reference program's by a relative error of at most 0.0039.
Values may be sent and summed in bfloat16 or wider, within the bound.
A program may use at most 128 MiB of HBM per device.

```python
import jax
import jax.numpy as jnp
from jax import lax

VIRT = 768
BASIS = 1024
AUX = 2048
STEPS = 2
NBLK = 8
OW = 4
N_GRP = 4


def draw_plan(key, part):
    others = jax.random.randint(jax.random.fold_in(key, 11), (2 * STEPS - 2,), 1, NBLK - 1)
    values = jnp.concatenate([jnp.array([0, NBLK - 1], jnp.int32), others.astype(jnp.int32)])
    order = jax.random.permutation(jax.random.fold_in(key, 23), 2 * STEPS)
    return values[order].reshape(STEPS, 2).astype(jnp.int32)


def block_levels(stream_key, extent, pieces, smallest, largest):
    def one(dim, blocks):
        heights = jax.random.uniform(jax.random.fold_in(jax.random.fold_in(stream_key, 6), dim), (blocks,), jnp.float32, smallest / len(pieces), largest / len(pieces))
        return jnp.repeat(jnp.exp(heights), extent[dim] // blocks).reshape((-1,) + (1,) * (len(extent) - dim - 1))

    loudness = one(*pieces[0])
    for cut in pieces[1:]:
        loudness = loudness * one(*cut)
    return loudness


def normal_values(own_key, shape, scale, most, pieces=(), held_as=jnp.bfloat16):
    values = jax.random.normal(own_key, shape, jnp.float32) * scale
    if len(pieces) > 0:
        values = block_levels(own_key, shape, pieces, -0.22, 0.18) * values
    return jnp.clip(values, min=-most, max=most).astype(held_as)


def setup_inputs(seed: int = 0) -> dict:
    keys = jax.random.split(jax.random.key(seed), 6)
    half_integrals = normal_values(keys[0], (NBLK, OW, BASIS, AUX), 0.08, 0.47851562, ((0, 8), (3, 4)))
    coeff_virtual = normal_values(keys[1], (BASIS, VIRT), BASIS ** -0.5, 0.1875)
    occ_energy = jnp.clip(jax.random.uniform(keys[2], (NBLK, OW), jnp.float32, -2.0, -0.3), -2.0, -0.3)
    vir_energy = jnp.clip(jax.random.uniform(keys[3], (VIRT,), jnp.float32, 0.2, 3.0), 0.2, 3.0)
    plan = draw_plan(jax.random.fold_in(keys[5], 71), 0)
    return dict(half_integrals=half_integrals, coeff_virtual=coeff_virtual, occ_energy=occ_energy, vir_energy=vir_energy, plan=plan)


def pair_terms(rows_i, rows_j, energy_i, energy_j, vir_energy):
    left = rows_i.astype(jnp.float32)
    right = rows_j.astype(jnp.float32)
    intersection = jnp.einsum("iap,jbp->ijab", left, right)
    denominator = (energy_i[:, None, None, None] + energy_j[None, :, None, None]
                   - vir_energy[None, None, :, None] - vir_energy[None, None, None, :])
    amplitude = intersection / denominator
    combined = (2.0 * amplitude - jnp.swapaxes(amplitude, 2, 3)).astype(jnp.bfloat16)
    return jnp.einsum("ijab,jbp->iap", combined.astype(jnp.float32), right)


def reference(half_integrals, coeff_virtual, occ_energy, vir_energy, plan):
    coeff_wide = coeff_virtual.astype(jnp.float32)

    def transform(block):
        return jnp.einsum("imp,ma->iap", block.astype(jnp.float32), coeff_wide).astype(jnp.bfloat16)

    rows_all = lax.map(transform, half_integrals)
    per_dev = OW // N_GRP
    grouped = rows_all.reshape(NBLK, N_GRP, per_dev, VIRT, AUX)
    energies = occ_energy.reshape(NBLK, N_GRP, per_dev)

    def one_group(flat_index):
        block_index = flat_index // N_GRP
        group_index = flat_index % N_GRP
        rows_i = grouped[block_index, group_index]
        energy_i = energies[block_index, group_index]
        total = jnp.zeros((per_dev, VIRT, AUX), jnp.float32)
        for step_index in range(STEPS):
            for slot_index in range(2):
                owner_index = plan[step_index, slot_index]
                rows_j = grouped[owner_index, group_index]
                energy_j = energies[owner_index, group_index]
                total = total + pair_terms(rows_i, rows_j, energy_i, energy_j, vir_energy)
        return total

    result = lax.map(one_group, jnp.arange(NBLK * N_GRP, dtype=jnp.int32))
    return result.reshape(NBLK, OW, VIRT, AUX)
```

```python
import functools

import jax
import jax.numpy as jnp
from jax import lax
from jax.experimental import pallas as pl
from jax.experimental.pallas import tpu as pltpu
from jax.sharding import PartitionSpec as P

MESH = pl.DeviceIdType.MESH


def kernel(
    n_grp, n_wide, slots, paths,
    owners, energy, trans, vir_col, vir_row,
    out,
    mine, sib, near, msg, far, owned, acc, comb, stage,
    local_sem, a2a_s, a2a_r, sib_s, sib_r, near_s, near_r, msg_s, msg_r, own_s, own_r, out_sem,
):
    g = lax.axis_index("grp")
    w = lax.axis_index("wide")
    virt, pb = mine.shape[1], mine.shape[2]
    half = virt // 2
    rb = half // paths
    bits = n_wide.bit_length() - 2
    core = lax.rem(w, 2)
    my_half = pl.multiple_of(core * half, 16)
    sib_half = pl.multiple_of((1 - core) * half, 16)

    def flip(index, bit):
        size = 1 << bit
        return index + size - 2 * size * lax.rem(lax.div(index, size), 2)

    def flip_grp(k):
        index = g
        for bit in range(n_grp.bit_length() - 1):
            if (k >> bit) & 1:
                index = flip(index, bit)
        return index

    def step_bit(h, t):
        return 1 + (h + t) % bits

    def remote(src, dst, send, recv, **device):
        return pltpu.make_async_remote_copy(
            src_ref=src, dst_ref=dst, send_sem=send, recv_sem=recv,
            device_id=device, device_id_type=MESH,
        )

    barrier = pltpu.get_barrier_semaphore()
    for bit in range(bits + 1):
        pl.semaphore_signal(
            barrier, inc=1, device_id={"wide": flip(w, bit)}, device_id_type=MESH
        )
    for k in range(1, n_grp):
        pl.semaphore_signal(
            barrier, inc=1, device_id={"grp": flip_grp(k)}, device_id_type=MESH
        )
    pl.semaphore_wait(barrier, bits + n_grp)

    sent = []

    def go(copy):
        copy.start()
        sent.append(copy)
        return copy

    a2a = [None]
    for k in range(1, n_grp):
        peer = flip_grp(k)
        a2a.append(go(remote(trans.at[peer], mine.at[k], a2a_s.at[k], a2a_r.at[k], grp=peer)))
    local = pltpu.make_async_copy(trans.at[g], mine.at[0], local_sem)
    local.start()
    local.wait()

    near_in, msg_in, own_in = {}, {}, {}

    def exchange_near(k):
        if k:
            a2a[k].wait_recv()
        pair = go(remote(
            mine.at[k, pl.ds(sib_half, half)], sib.at[k], sib_s.at[k], sib_r.at[k], wide=flip(w, 0)
        ))
        for h in range(paths):
            peer = flip(w, step_bit(h, 0))
            rows = pl.ds(pl.multiple_of(my_half + h * rb, 16), rb)
            near_in[k, h, 0] = go(remote(
                mine.at[k, rows], near.at[k, h, 0], near_s.at[k, h, 0], near_r.at[k, h, 0], wide=peer
            ))
        pair.wait_recv()
        for h in range(paths):
            peer = flip(w, step_bit(h, 0))
            near_in[k, h, 1] = go(remote(
                sib.at[k, pl.ds(h * rb, rb)], near.at[k, h, 1],
                near_s.at[k, h, 1], near_r.at[k, h, 1], wide=peer,
            ))

    def same(owner, index):
        return owner == index

    def in_far(owner, h, t):
        inside = [0] + [step_bit(h, u) for u in range(t)]
        there = flip(w, step_bit(h, t))
        ok = None
        for bit in range(bits + 1):
            if bit in inside:
                continue
            agree = lax.rem(lax.div(owner, 1 << bit), 2) == lax.rem(lax.div(there, 1 << bit), 2)
            ok = agree if ok is None else jnp.logical_and(ok, agree)
        return ok

    def pick(k, h, t, r, who, unit):
        rows = 32 if rb % 32 == 0 else 16
        at = pl.multiple_of(r * rows, rows)
        value = mine[k, pl.ds(pl.multiple_of(my_half + h * rb + at, 16), rows), :]
        first = flip(w, step_bit(h, 0))
        choices = [
            (flip(w, 0), lambda: sib[k, pl.ds(pl.multiple_of(h * rb + at, 16), rows), :]),
            (first, lambda: near[k, h, 0, pl.ds(at, rows), :]),
            (flip(first, 0), lambda: near[k, h, 1, pl.ds(at, rows), :]),
        ]
        for index, load in choices:
            for owner in who:
                value = lax.select(same(owner, index), load(), value)
        for u in range(1, t):
            for owner in who:
                value = lax.select(
                    in_far(owner, h, u), far[k, h, u - 1, unit, pl.ds(at, rows), :], value
                )
        return value

    def row_loop(body):
        rows = 32 if rb % 32 == 0 else 16

        @pl.loop(0, rb // rows)
        def _(r):
            body(r, pl.multiple_of(r * rows, rows), rows)

    def exchange_far(k, t):
        for h in range(paths):
            if t == 1:
                near_in[k, h, 0].wait_recv()
                near_in[k, h, 1].wait_recv()
            else:
                msg_in[k, h, t - 1].wait_recv()

            def body(r, at, rows):
                for unit in range(slots - 1):
                    who = [0, n_wide - 1] if unit == 0 else [owners[unit]]
                    msg[k, h, t - 1, unit, pl.ds(at, rows), :] = pick(k, h, t, r, who, unit)

            row_loop(body)
            msg_in[k, h, t] = go(remote(
                msg.at[k, h, t - 1], far.at[k, h, t - 1],
                msg_s.at[k, h, t - 1], msg_r.at[k, h, t - 1], wide=flip(w, step_bit(h, t)),
            ))

    def to_sibling(k):
        for h in range(paths):
            msg_in[k, h, bits - 1].wait_recv()

            def body(r, at, rows):
                for s in range(slots):
                    unit = 0 if s in (0, slots - 1) else s
                    who = {0: 0, slots - 1: n_wide - 1}.get(s)
                    who = owners[s] if who is None else who
                    owned[k, s, pl.ds(pl.multiple_of(my_half + h * rb + at, 16), rows), :] = pick(
                        k, h, bits, r, [who], unit
                    )

            row_loop(body)
        part = owned.at[k, :, pl.ds(my_half, half), :]
        own_in[k] = go(remote(part, part, own_s.at[k], own_r.at[k], wide=flip(w, 0)))

    tile = 256 if virt % 256 == 0 else virt
    contract = (((1,), (1,)), ((), ()))

    def intersect(k):
        own_in[k].wait_recv()

        @pl.loop(0, slots)
        def _(s):
            @pl.loop(0, virt // tile)
            def _(r):
                rows = pl.ds(pl.multiple_of(r * tile, tile), tile)
                straight = lax.dot_general(
                    mine[k, rows, :], owned[k, s], contract, preferred_element_type=jnp.float32
                )
                turned = lax.dot_general(
                    owned[k, s, rows, :], mine[k], contract, preferred_element_type=jnp.float32
                )
                value = 2.0 * straight - turned
                if k:
                    value = value + acc[s, rows, :]
                acc[s, rows, :] = value

    exchange_near(0)
    for t in range(1, bits):
        exchange_far(0, t)
    for k in range(n_grp):
        if k + 1 < n_grp:
            exchange_near(k + 1)
        to_sibling(k)
        if k + 1 < n_grp:
            for t in range(1, bits):
                exchange_far(k + 1, t)
        intersect(k)

    for s in range(slots):
        total = energy[s]

        @pl.loop(0, virt // tile)
        def _(r):
            rows = pl.ds(pl.multiple_of(r * tile, tile), tile)
            denominator = (total - vir_col[rows, :]) - vir_row[...]
            comb[rows, pl.ds(s * virt, virt)] = (acc[s, rows, :] / denominator).astype(jnp.bfloat16)

    outs = []
    for k in range(n_grp):
        if k >= 2:
            outs[k - 2].wait()

        @pl.loop(0, virt // tile)
        def _(r):
            rows = pl.ds(pl.multiple_of(r * tile, tile), tile)
            stage[k % 2, rows, :] = jnp.dot(
                comb[rows, :], owned[k].reshape(slots * virt, pb),
                preferred_element_type=jnp.float32,
            )

        columns = pl.ds(pl.multiple_of(flip_grp(k) * pb, 128), pb)
        copy = pltpu.make_async_copy(stage.at[k % 2], out.at[:, columns], out_sem.at[k % 2])
        copy.start()
        outs.append(copy)
    for copy in outs[-2:]:
        copy.wait()
    for copy in sent:
        copy.wait_send()


def shards(n_grp, n_wide, half_integrals, coeff_virtual, occ_energy, vir_energy, plan):
    trans = jnp.einsum(
        "imp,ma->iap", half_integrals[0], coeff_virtual, preferred_element_type=jnp.float32
    ).astype(jnp.bfloat16)
    virt, pb = trans.shape[1:]
    owners = jnp.sort(plan.reshape(-1))
    slots = owners.shape[0]
    orbital = lax.axis_index("grp")
    energy = occ_energy[lax.axis_index("wide"), orbital] + occ_energy[owners, orbital]
    bits = n_wide.bit_length() - 2
    paths = bits if virt % (32 * bits) == 0 else 1
    rb = virt // 2 // paths
    bf16, f32 = jnp.bfloat16, jnp.float32
    dma = pltpu.SemaphoreType.DMA
    smem = pl.BlockSpec(memory_space=pltpu.SMEM)
    vmem = pl.BlockSpec(memory_space=pltpu.VMEM)
    hbm = pl.BlockSpec(memory_space=pl.ANY)
    flops = 3 * 2 * slots * virt * virt * pb * n_grp
    density = pl.pallas_call(
        functools.partial(kernel, n_grp, n_wide, slots, paths),
        out_shape=jax.ShapeDtypeStruct((virt, pb * n_grp), f32),
        in_specs=[smem, smem, hbm, vmem, vmem],
        out_specs=hbm,
        scratch_shapes=[
            pltpu.VMEM((n_grp, virt, pb), bf16),
            pltpu.VMEM((n_grp, virt // 2, pb), bf16),
            pltpu.VMEM((n_grp, paths, 2, rb, pb), bf16),
            pltpu.VMEM((n_grp, paths, bits - 1, slots - 1, rb, pb), bf16),
            pltpu.VMEM((n_grp, paths, bits - 1, slots - 1, rb, pb), bf16),
            pltpu.VMEM((n_grp, slots, virt, pb), bf16),
            pltpu.VMEM((slots, virt, virt), f32),
            pltpu.VMEM((virt, slots * virt), bf16),
            pltpu.VMEM((2, virt, pb), f32),
            dma(()),
            dma((n_grp,)), dma((n_grp,)),
            dma((n_grp,)), dma((n_grp,)),
            dma((n_grp, paths, 2)), dma((n_grp, paths, 2)),
            dma((n_grp, paths, bits - 1)), dma((n_grp, paths, bits - 1)),
            dma((n_grp,)), dma((n_grp,)),
            dma((2,)),
        ],
        compiler_params=pltpu.CompilerParams(
            collective_id=0, has_side_effects=True, vmem_limit_bytes=63 * 1024 * 1024
        ),
        cost_estimate=pl.CostEstimate(
            flops=flops, bytes_accessed=16 * virt * pb * n_grp, transcendentals=0
        ),
    )(owners, energy, trans, vir_energy[:, None], vir_energy[None, :])
    return density[None, None]


def solution(mesh):
    return jax.shard_map(
        functools.partial(shards, mesh.shape["grp"], mesh.shape["wide"]),
        mesh=mesh,
        in_specs=(P("wide", None, None, "grp"), P(), P(), P(), P()),
        out_specs=P("wide", "grp", None, None),
        check_vma=False,
    )
```

```python
import functools

import jax
import jax.numpy as jnp
from jax import lax
from jax.experimental import pallas as pl
from jax.experimental.pallas import tpu as pltpu
from jax.sharding import PartitionSpec as P

MESH = pl.DeviceIdType.MESH


def kernel(
    n_grp, n_wide, slots, paths,
    owners, energy, trans, vir_col, vir_row,
    out,
    mine, sib, near, msg, far, owned, acc, comb, stage,
    local_sem, a2a_s, a2a_r, sib_s, sib_r, near_s, near_r, msg_s, msg_r, own_s, own_r, out_sem,
):
    g = lax.axis_index("grp")
    w = lax.axis_index("wide")
    virt, pb = mine.shape[1], mine.shape[2]
    half = virt // 2
    rb = half // paths
    bits = n_wide.bit_length() - 2
    core = lax.rem(w, 2)
    my_half = pl.multiple_of(core * half, 16)
    sib_half = pl.multiple_of((1 - core) * half, 16)

    def flip(index, bit):
        size = 1 << bit
        return index + size - 2 * size * lax.rem(lax.div(index, size), 2)

    def flip_grp(k):
        index = g
        for bit in range(n_grp.bit_length() - 1):
            if (k >> bit) & 1:
                index = flip(index, bit)
        return index

    def step_bit(h, t):
        return 1 + (h + t) % bits

    def remote(src, dst, send, recv, **device):
        return pltpu.make_async_remote_copy(
            src_ref=src, dst_ref=dst, send_sem=send, recv_sem=recv,
            device_id=device, device_id_type=MESH,
        )

    barrier = pltpu.get_barrier_semaphore()
    for bit in range(bits + 1):
        pl.semaphore_signal(
            barrier, inc=1, device_id={"wide": flip(w, bit)}, device_id_type=MESH
        )
    for k in range(1, n_grp):
        pl.semaphore_signal(
            barrier, inc=1, device_id={"grp": flip_grp(k)}, device_id_type=MESH
        )
    pl.semaphore_wait(barrier, bits + n_grp)

    sent = []

    def go(copy):
        copy.start()
        sent.append(copy)
        return copy

    middle = lax.rem(lax.div(g + 1, 2), 2) if n_grp >= 4 else 0

    def place(k):
        if n_grp < 4 or k % 4 < 2:
            return k
        return k + middle * (1 - 2 * (k % 2))

    def slice_of(k):
        if n_grp < 4 or k % 4 < 2:
            return flip_grp(k)
        return flip_grp(k) + middle * (flip_grp(k ^ 1) - flip_grp(k))

    a2a = [None]
    for k in range(1, n_grp):
        peer = flip_grp(k)
        a2a.append(remote(trans.at[peer], mine.at[k], a2a_s.at[k], a2a_r.at[k], grp=peer))

    def first_sends():
        a2a[1].start()
        if n_grp >= 4:
            pl.when(middle == 1)(a2a[3].start)

    def second_sends():
        a2a[1].wait_send()
        if n_grp >= 4:
            pl.when(middle == 1)(a2a[3].wait_send)
            a2a[2].start()
        for k in range(4, n_grp):
            go(a2a[k])

    def third_sends():
        if n_grp >= 4:
            a2a[2].wait_send()

            a2a[3].start()

    first_sends()
    local = pltpu.make_async_copy(trans.at[g], mine.at[0], local_sem)
    local.start()
    local.wait()

    near_in, msg_in, own_in = {}, {}, {}

    def exchange_near(k):
        at = place(k)
        if k:
            arrived = mine.at[at]
            pltpu.make_async_copy(arrived, arrived, a2a_r.at[at]).wait()
        if k == 2:
            pl.when(middle == 0)(third_sends)
        pair = go(remote(
            mine.at[at, pl.ds(sib_half, half)], sib.at[k], sib_s.at[k], sib_r.at[k], wide=flip(w, 0)
        ))
        for h in range(paths):
            peer = flip(w, step_bit(h, 0))
            rows = pl.ds(pl.multiple_of(my_half + h * rb, 16), rb)
            near_in[k, h, 0] = go(remote(
                mine.at[at, rows], near.at[k, h, 0], near_s.at[k, h, 0], near_r.at[k, h, 0], wide=peer
            ))
        pair.wait_recv()
        for h in range(paths):
            peer = flip(w, step_bit(h, 0))
            near_in[k, h, 1] = go(remote(
                sib.at[k, pl.ds(h * rb, rb)], near.at[k, h, 1],
                near_s.at[k, h, 1], near_r.at[k, h, 1], wide=peer,
            ))

    def same(owner, index):
        return owner == index

    def in_far(owner, h, t):
        inside = [0] + [step_bit(h, u) for u in range(t)]
        there = flip(w, step_bit(h, t))
        ok = None
        for bit in range(bits + 1):
            if bit in inside:
                continue
            agree = lax.rem(lax.div(owner, 1 << bit), 2) == lax.rem(lax.div(there, 1 << bit), 2)
            ok = agree if ok is None else jnp.logical_and(ok, agree)
        return ok

    def pick(k, h, t, r, who, unit):
        rows = 32 if rb % 32 == 0 else 16
        at = pl.multiple_of(r * rows, rows)
        value = mine[place(k), pl.ds(pl.multiple_of(my_half + h * rb + at, 16), rows), :]
        first = flip(w, step_bit(h, 0))
        choices = [
            (flip(w, 0), lambda: sib[k, pl.ds(pl.multiple_of(h * rb + at, 16), rows), :]),
            (first, lambda: near[k, h, 0, pl.ds(at, rows), :]),
            (flip(first, 0), lambda: near[k, h, 1, pl.ds(at, rows), :]),
        ]
        for index, load in choices:
            for owner in who:
                value = lax.select(same(owner, index), load(), value)
        for u in range(1, t):
            for owner in who:
                value = lax.select(
                    in_far(owner, h, u), far[k, h, u - 1, unit, pl.ds(at, rows), :], value
                )
        return value

    def row_loop(body):
        rows = 32 if rb % 32 == 0 else 16

        @pl.loop(0, rb // rows)
        def _(r):
            body(r, pl.multiple_of(r * rows, rows), rows)

    def exchange_far(k, t):
        for h in range(paths):
            if t == 1:
                near_in[k, h, 0].wait_recv()
                near_in[k, h, 1].wait_recv()
            else:
                msg_in[k, h, t - 1].wait_recv()

            def body(r, at, rows):
                for unit in range(slots - 1):
                    who = [0, n_wide - 1] if unit == 0 else [owners[unit]]
                    msg[k, h, t - 1, unit, pl.ds(at, rows), :] = pick(k, h, t, r, who, unit)

            row_loop(body)
            msg_in[k, h, t] = go(remote(
                msg.at[k, h, t - 1], far.at[k, h, t - 1],
                msg_s.at[k, h, t - 1], msg_r.at[k, h, t - 1], wide=flip(w, step_bit(h, t)),
            ))

    def to_sibling(k):
        for h in range(paths):
            msg_in[k, h, bits - 1].wait_recv()

            def body(r, at, rows):
                for s in range(slots):
                    unit = 0 if s in (0, slots - 1) else s
                    who = {0: 0, slots - 1: n_wide - 1}.get(s)
                    who = owners[s] if who is None else who
                    owned[k, s, pl.ds(pl.multiple_of(my_half + h * rb + at, 16), rows), :] = pick(
                        k, h, bits, r, [who], unit
                    )

            row_loop(body)
        part = owned.at[k, :, pl.ds(my_half, half), :]
        own_in[k] = go(remote(part, part, own_s.at[k], own_r.at[k], wide=flip(w, 0)))

    tile = 256 if virt % 256 == 0 else virt
    contract = (((1,), (1,)), ((), ()))

    def intersect(k):
        own_in[k].wait_recv()

        @pl.loop(0, slots)
        def _(s):
            @pl.loop(0, virt // tile)
            def _(r):
                rows = pl.ds(pl.multiple_of(r * tile, tile), tile)
                straight = lax.dot_general(
                    mine[place(k), rows, :], owned[k, s], contract, preferred_element_type=jnp.float32
                )
                turned = lax.dot_general(
                    owned[k, s, rows, :], mine[place(k)], contract, preferred_element_type=jnp.float32
                )
                value = 2.0 * straight - turned
                if k:
                    value = value + acc[s, rows, :]
                acc[s, rows, :] = value

    exchange_near(0)
    for t in range(1, bits):
        exchange_far(0, t)
    second_sends()
    for k in range(n_grp):
        if k + 1 < n_grp:
            exchange_near(k + 1)
        to_sibling(k)
        if k + 1 < n_grp:
            for t in range(1, bits):
                exchange_far(k + 1, t)
        intersect(k)

    for s in range(slots):
        total = energy[s]

        @pl.loop(0, virt // tile)
        def _(r):
            rows = pl.ds(pl.multiple_of(r * tile, tile), tile)
            denominator = (total - vir_col[rows, :]) - vir_row[...]
            comb[rows, pl.ds(s * virt, virt)] = (acc[s, rows, :] / denominator).astype(jnp.bfloat16)

    outs = []
    for k in range(n_grp):
        if k >= 2:
            outs[k - 2].wait()

        @pl.loop(0, virt // tile)
        def _(r):
            rows = pl.ds(pl.multiple_of(r * tile, tile), tile)
            stage[k % 2, rows, :] = jnp.dot(
                comb[rows, :], owned[k].reshape(slots * virt, pb),
                preferred_element_type=jnp.float32,
            )

        columns = pl.ds(pl.multiple_of(slice_of(k) * pb, 128), pb)
        copy = pltpu.make_async_copy(stage.at[k % 2], out.at[:, columns], out_sem.at[k % 2])
        copy.start()
        outs.append(copy)
    for copy in outs[-2:]:
        copy.wait()
    if n_grp >= 4:
        pl.when(middle == 1)(a2a[2].wait_send)
        pl.when(middle == 0)(a2a[3].wait_send)
    for copy in sent:
        copy.wait_send()


def shards(n_grp, n_wide, half_integrals, coeff_virtual, occ_energy, vir_energy, plan):
    trans = jnp.einsum(
        "imp,ma->iap", half_integrals[0], coeff_virtual, preferred_element_type=jnp.float32
    ).astype(jnp.bfloat16)
    virt, pb = trans.shape[1:]
    owners = jnp.sort(plan.reshape(-1))
    slots = owners.shape[0]
    orbital = lax.axis_index("grp")
    energy = occ_energy[lax.axis_index("wide"), orbital] + occ_energy[owners, orbital]
    bits = n_wide.bit_length() - 2
    paths = bits if virt % (32 * bits) == 0 else 1
    rb = virt // 2 // paths
    bf16, f32 = jnp.bfloat16, jnp.float32
    dma = pltpu.SemaphoreType.DMA
    smem = pl.BlockSpec(memory_space=pltpu.SMEM)
    vmem = pl.BlockSpec(memory_space=pltpu.VMEM)
    hbm = pl.BlockSpec(memory_space=pl.ANY)
    flops = 3 * 2 * slots * virt * virt * pb * n_grp
    density = pl.pallas_call(
        functools.partial(kernel, n_grp, n_wide, slots, paths),
        out_shape=jax.ShapeDtypeStruct((virt, pb * n_grp), f32),
        in_specs=[smem, smem, hbm, vmem, vmem],
        out_specs=hbm,
        scratch_shapes=[
            pltpu.VMEM((n_grp, virt, pb), bf16),
            pltpu.VMEM((n_grp, virt // 2, pb), bf16),
            pltpu.VMEM((n_grp, paths, 2, rb, pb), bf16),
            pltpu.VMEM((n_grp, paths, bits - 1, slots - 1, rb, pb), bf16),
            pltpu.VMEM((n_grp, paths, bits - 1, slots - 1, rb, pb), bf16),
            pltpu.VMEM((n_grp, slots, virt, pb), bf16),
            pltpu.VMEM((slots, virt, virt), f32),
            pltpu.VMEM((virt, slots * virt), bf16),
            pltpu.VMEM((2, virt, pb), f32),
            dma(()),
            dma((n_grp,)), dma((n_grp,)),
            dma((n_grp,)), dma((n_grp,)),
            dma((n_grp, paths, 2)), dma((n_grp, paths, 2)),
            dma((n_grp, paths, bits - 1)), dma((n_grp, paths, bits - 1)),
            dma((n_grp,)), dma((n_grp,)),
            dma((2,)),
        ],
        compiler_params=pltpu.CompilerParams(
            collective_id=0, has_side_effects=True, vmem_limit_bytes=63 * 1024 * 1024
        ),
        cost_estimate=pl.CostEstimate(
            flops=flops, bytes_accessed=16 * virt * pb * n_grp, transcendentals=0
        ),
    )(owners, energy, trans, vir_energy[:, None], vir_energy[None, :])
    return density[None, None]


def solution(mesh):
    return jax.shard_map(
        functools.partial(shards, mesh.shape["grp"], mesh.shape["wide"]),
        mesh=mesh,
        in_specs=(P("wide", None, None, "grp"), P(), P(), P(), P()),
        out_specs=P("wide", "grp", None, None),
        check_vma=False,
    )
```

```python
import functools

import jax
import jax.numpy as jnp
from jax import lax
from jax.experimental import pallas as pl
from jax.experimental.pallas import tpu as pltpu
from jax.sharding import PartitionSpec as P

MESH = pl.DeviceIdType.MESH


def kernel(
    n_grp, n_wide, slots, paths,
    plan, occ, vir, coeff, half_integrals,
    comb_out, owned_out,
    mine, sib, near, msg, far, owned, acc, comb, trans, taken, coeff_t, vir_col,
    taken_sem, a2a_s, a2a_r, sib_s, sib_r, near_s, near_r, msg_s, msg_r, own_s, own_r, owned_sem, comb_sem,
):
    g = lax.axis_index("grp")
    w = lax.axis_index("wide")
    virt, pb = mine.shape[1], mine.shape[2]
    half = virt // 2
    rb = half // paths
    bits = n_wide.bit_length() - 2
    core = lax.rem(w, 2)
    my_half = pl.multiple_of(core * half, 16)
    sib_half = pl.multiple_of((1 - core) * half, 16)

    def flip(index, bit):
        size = 1 << bit
        return index + size - 2 * size * lax.rem(lax.div(index, size), 2)

    def flip_grp(k):
        index = g
        for bit in range(n_grp.bit_length() - 1):
            if (k >> bit) & 1:
                index = flip(index, bit)
        return index

    def step_bit(h, t):
        return 1 + (h + t) % bits

    def remote(src, dst, send, recv, **device):
        return pltpu.make_async_remote_copy(
            src_ref=src, dst_ref=dst, send_sem=send, recv_sem=recv,
            device_id=device, device_id_type=MESH,
        )

    order = [0, 1, 3, 2] if n_grp >= 4 else [0, 1]
    order = order + list(range(len(order), n_grp))

    def take(i):
        return pltpu.make_async_copy(
            half_integrals.at[0, flip_grp(order[i])], taken.at[i % 2], taken_sem.at[i % 2]
        )

    take(0).start()
    barrier = pltpu.get_barrier_semaphore()
    for bit in range(bits + 1):
        pl.semaphore_signal(
            barrier, inc=1, device_id={"wide": flip(w, bit)}, device_id_type=MESH
        )
    for k in range(1, n_grp):
        pl.semaphore_signal(
            barrier, inc=1, device_id={"grp": flip_grp(k)}, device_id_type=MESH
        )

    owners = [plan[a, b] for a in range(plan.shape[0]) for b in range(plan.shape[1])]
    for last in range(slots - 1, 0, -1):
        for a in range(last):
            low = jnp.minimum(owners[a], owners[a + 1])
            owners[a + 1] = jnp.maximum(owners[a], owners[a + 1])
            owners[a] = low

    tile = 256 if virt % 256 == 0 else virt

    @pl.loop(0, virt // 128)
    def _(c):
        columns = pl.ds(pl.multiple_of(c * 128, 128), 128)
        coeff_t[columns, :] = coeff[:, columns].T

    def transform(i, rows_of):
        if i + 1 < n_grp:
            take(i + 1).start()
        take(i).wait()

        @pl.loop(0, virt // tile)
        def _(r):
            rows = pl.ds(pl.multiple_of(r * tile, tile), tile)
            rows_of[rows, :] = jnp.dot(
                coeff_t[rows, :], taken[i % 2], preferred_element_type=jnp.float32
            ).astype(jnp.bfloat16)

    transform(0, mine.at[0])
    pl.semaphore_wait(barrier, bits + n_grp)

    sent = []

    def go(copy):
        copy.start()
        sent.append(copy)
        return copy

    middle = lax.rem(lax.div(g + 1, 2), 2) if n_grp >= 4 else 0

    def place(k):
        if n_grp < 4 or k % 4 < 2:
            return k
        return k + middle * (1 - 2 * (k % 2))

    def slice_of(k):
        if n_grp < 4 or k % 4 < 2:
            return flip_grp(k)
        return flip_grp(k) + middle * (flip_grp(k ^ 1) - flip_grp(k))

    a2a = [None]
    for k in range(1, n_grp):
        peer = flip_grp(k)
        a2a.append(remote(trans.at[k], mine.at[k], a2a_s.at[k], a2a_r.at[k], grp=peer))

    def second_sends():
        a2a[1].wait_send()
        if n_grp >= 4:
            pl.when(middle == 1)(a2a[3].wait_send)
            a2a[2].start()
        for k in range(4, n_grp):
            go(a2a[k])

    def third_sends():
        if n_grp >= 4:
            a2a[2].wait_send()

            a2a[3].start()

    near_in, msg_in, own_in = {}, {}, {}

    def start_near(k):
        at = place(k)
        if k:
            arrived = mine.at[at]
            pltpu.make_async_copy(arrived, arrived, a2a_r.at[at]).wait()
        if k == 2:
            pl.when(middle == 0)(third_sends)
        near_in[k] = go(remote(
            mine.at[at, pl.ds(sib_half, half)], sib.at[k], sib_s.at[k], sib_r.at[k], wide=flip(w, 0)
        ))
        for h in range(paths):
            peer = flip(w, step_bit(h, 0))
            rows = pl.ds(pl.multiple_of(my_half + h * rb, 16), rb)
            near_in[k, h, 0] = go(remote(
                mine.at[at, rows], near.at[k, h, 0], near_s.at[k, h, 0], near_r.at[k, h, 0], wide=peer
            ))

    def finish_near(k):
        near_in[k].wait_recv()
        for h in range(paths):
            peer = flip(w, step_bit(h, 0))
            near_in[k, h, 1] = go(remote(
                sib.at[k, pl.ds(h * rb, rb)], near.at[k, h, 1],
                near_s.at[k, h, 1], near_r.at[k, h, 1], wide=peer,
            ))

    def same(owner, index):
        return owner == index

    def in_far(owner, h, t):
        inside = [0] + [step_bit(h, u) for u in range(t)]
        there = flip(w, step_bit(h, t))
        ok = None
        for bit in range(bits + 1):
            if bit in inside:
                continue
            agree = lax.rem(lax.div(owner, 1 << bit), 2) == lax.rem(lax.div(there, 1 << bit), 2)
            ok = agree if ok is None else jnp.logical_and(ok, agree)
        return ok

    def pick(k, h, t, r, who, unit):
        rows = 32 if rb % 32 == 0 else 16
        at = pl.multiple_of(r * rows, rows)
        value = mine[place(k), pl.ds(pl.multiple_of(my_half + h * rb + at, 16), rows), :]
        first = flip(w, step_bit(h, 0))
        choices = [
            (flip(w, 0), lambda: sib[k, pl.ds(pl.multiple_of(h * rb + at, 16), rows), :]),
            (first, lambda: near[k, h, 0, pl.ds(at, rows), :]),
            (flip(first, 0), lambda: near[k, h, 1, pl.ds(at, rows), :]),
        ]
        for index, load in choices:
            for owner in who:
                value = lax.select(same(owner, index), load(), value)
        for u in range(1, t):
            for owner in who:
                value = lax.select(
                    in_far(owner, h, u), far[k, h, u - 1, unit, pl.ds(at, rows), :], value
                )
        return value

    def row_loop(body):
        rows = 32 if rb % 32 == 0 else 16

        @pl.loop(0, rb // rows)
        def _(r):
            body(r, pl.multiple_of(r * rows, rows), rows)

    def exchange_far(k, t):
        for h in range(paths):
            if t == 1:
                near_in[k, h, 0].wait_recv()
                near_in[k, h, 1].wait_recv()
            else:
                msg_in[k, h, t - 1].wait_recv()

            def body(r, at, rows):
                for unit in range(slots - 1):
                    who = [0, n_wide - 1] if unit == 0 else [owners[unit]]
                    msg[k, h, t - 1, unit, pl.ds(at, rows), :] = pick(k, h, t, r, who, unit)

            row_loop(body)
            msg_in[k, h, t] = go(remote(
                msg.at[k, h, t - 1], far.at[k, h, t - 1],
                msg_s.at[k, h, t - 1], msg_r.at[k, h, t - 1], wide=flip(w, step_bit(h, t)),
            ))

    def to_sibling(k):
        for h in range(paths):
            msg_in[k, h, bits - 1].wait_recv()

            def body(r, at, rows):
                for s in range(slots):
                    unit = 0 if s in (0, slots - 1) else s
                    who = {0: 0, slots - 1: n_wide - 1}.get(s)
                    who = owners[s] if who is None else who
                    owned[k, s, pl.ds(pl.multiple_of(my_half + h * rb + at, 16), rows), :] = pick(
                        k, h, bits, r, [who], unit
                    )

            row_loop(body)
        part = owned.at[k, :, pl.ds(my_half, half), :]
        own_in[k] = go(remote(part, part, own_s.at[k], own_r.at[k], wide=flip(w, 0)))

    contract = (((1,), (1,)), ((), ()))

    def intersect(k):
        own_in[k].wait_recv()
        columns = pl.ds(pl.multiple_of(slice_of(k) * pb, 128), pb)
        outs.append(pltpu.make_async_copy(
            owned.at[k], owned_out.at[:, :, columns], owned_sem.at[k]
        ))
        outs[-1].start()

        @pl.loop(0, slots)
        def _(s):
            @pl.loop(0, virt // tile)
            def _(r):
                rows = pl.ds(pl.multiple_of(r * tile, tile), tile)
                straight = lax.dot_general(
                    mine[place(k), rows, :], owned[k, s], contract, preferred_element_type=jnp.float32
                )
                turned = lax.dot_general(
                    owned[k, s, rows, :], mine[place(k)], contract, preferred_element_type=jnp.float32
                )
                value = 2.0 * straight - turned
                if k:
                    value = value + acc[s, rows, :]
                acc[s, rows, :] = value

    outs = []
    start_near(0)
    transform(1, trans.at[1])
    a2a[1].start()
    finish_near(0)
    for i in range(2, n_grp):
        transform(i, trans.at[order[i]])
        if order[i] == 3:
            pl.when(middle == 1)(a2a[3].start)

    @pl.loop(0, virt // 128)
    def _(c):
        part = pl.ds(pl.multiple_of(c * 128, 128), 128)
        vir_col[part, :] = jnp.broadcast_to(vir[part].reshape(1, 128), (128, 128)).T

    for t in range(1, bits):
        exchange_far(0, t)
    second_sends()
    for k in range(n_grp):
        if k + 1 < n_grp:
            start_near(k + 1)
            finish_near(k + 1)
        to_sibling(k)
        if k + 1 < n_grp:
            for t in range(1, bits):
                exchange_far(k + 1, t)
        intersect(k)

    for s in range(slots):
        total = occ[g, w] + occ[g, owners[s]]
        part = pl.ds(s * virt, virt)

        @pl.loop(0, virt // tile)
        def _(r):
            rows = pl.ds(pl.multiple_of(r * tile, tile), tile)
            denominator = (total - vir_col[rows, :1]) - vir[...].reshape(1, virt)
            comb[rows, part] = (acc[s, rows, :] / denominator).astype(jnp.bfloat16)

        outs.append(pltpu.make_async_copy(comb.at[:, part], comb_out.at[:, part], comb_sem.at[s]))
        outs[-1].start()
    for copy in outs:
        copy.wait()
    if n_grp >= 4:
        pl.when(middle == 1)(a2a[2].wait_send)
        pl.when(middle == 0)(a2a[3].wait_send)
    for copy in sent:
        copy.wait_send()


def shards(n_grp, n_wide, half_integrals, coeff_virtual, occ_energy, vir_energy, plan):
    basis, virt = coeff_virtual.shape
    pb = half_integrals.shape[3]
    slots = plan.size
    bits = n_wide.bit_length() - 2
    paths = bits if virt % (32 * bits) == 0 else 1
    rb = virt // 2 // paths
    bf16, f32 = jnp.bfloat16, jnp.float32
    dma = pltpu.SemaphoreType.DMA
    smem = pl.BlockSpec(memory_space=pltpu.SMEM)
    vmem = pl.BlockSpec(memory_space=pltpu.VMEM)
    hbm = pl.BlockSpec(memory_space=pl.ANY)
    flops = 2 * 2 * slots * virt * virt * pb * n_grp
    comb, owned = pl.pallas_call(
        functools.partial(kernel, n_grp, n_wide, slots, paths),
        out_shape=[
            jax.ShapeDtypeStruct((virt, slots * virt), bf16),
            jax.ShapeDtypeStruct((slots, virt, n_grp * pb), bf16),
        ],
        in_specs=[smem, smem, vmem, vmem, hbm],
        out_specs=[hbm, hbm],
        scratch_shapes=[
            pltpu.VMEM((n_grp, virt, pb), bf16),
            pltpu.VMEM((n_grp, virt // 2, pb), bf16),
            pltpu.VMEM((n_grp, paths, 2, rb, pb), bf16),
            pltpu.VMEM((n_grp, paths, bits - 1, slots - 1, rb, pb), bf16),
            pltpu.VMEM((n_grp, paths, bits - 1, slots - 1, rb, pb), bf16),
            pltpu.VMEM((n_grp, slots, virt, pb), bf16),
            pltpu.VMEM((slots, virt, virt), f32),
            pltpu.VMEM((virt, slots * virt), bf16),
            pltpu.VMEM((n_grp, virt, pb), bf16),
            pltpu.VMEM((2, basis, pb), bf16),
            pltpu.VMEM((virt, basis), bf16),
            pltpu.VMEM((virt, 128), f32),
            dma((2,)),
            dma((n_grp,)), dma((n_grp,)),
            dma((n_grp,)), dma((n_grp,)),
            dma((n_grp, paths, 2)), dma((n_grp, paths, 2)),
            dma((n_grp, paths, bits - 1)), dma((n_grp, paths, bits - 1)),
            dma((n_grp,)), dma((n_grp,)),
            dma((n_grp,)), dma((slots,)),
        ],
        compiler_params=pltpu.CompilerParams(
            collective_id=0, has_side_effects=True, vmem_limit_bytes=63 * 1024 * 1024
        ),
        cost_estimate=pl.CostEstimate(
            flops=flops, bytes_accessed=16 * virt * pb * n_grp, transcendentals=0
        ),
    )(plan, occ_energy.T, vir_energy, coeff_virtual, half_integrals)
    density = jnp.dot(
        comb, owned.reshape(slots * virt, n_grp * pb), preferred_element_type=jnp.float32
    )
    return density[None, None]


def solution(mesh):
    return jax.shard_map(
        functools.partial(shards, mesh.shape["grp"], mesh.shape["wide"]),
        mesh=mesh,
        in_specs=(P("wide", None, None, "grp"), P(), P(), P(), P()),
        out_specs=P("wide", "grp", None, None),
        check_vma=False,
    )
```

```python
import functools

import jax
import jax.numpy as jnp
from jax import lax
from jax.experimental import pallas as pl
from jax.experimental.pallas import tpu as pltpu
from jax.sharding import PartitionSpec as P

MESH = pl.DeviceIdType.MESH


def kernel(
    n_grp, n_wide, slots, paths,
    plan, occ, vir, coeff, half_integrals,
    comb_out, owned_out,
    mine, sib, near, msg, far, owned, acc, comb, trans, taken, coeff_t, vir_col,
    taken_sem, a2a_s, a2a_r, sib_s, sib_r, near_s, near_r, msg_s, msg_r, own_s, own_r, owned_sem, comb_sem,
):
    g = lax.axis_index("grp")
    w = lax.axis_index("wide")
    virt, pb = mine.shape[1], mine.shape[2]
    half = virt // 2
    rb = half // paths
    bits = n_wide.bit_length() - 2
    core = lax.rem(w, 2)
    my_half = pl.multiple_of(core * half, 16)
    sib_half = pl.multiple_of((1 - core) * half, 16)

    def flip(index, bit):
        size = 1 << bit
        return index + size - 2 * size * lax.rem(lax.div(index, size), 2)

    def flip_grp(k):
        index = g
        for bit in range(n_grp.bit_length() - 1):
            if (k >> bit) & 1:
                index = flip(index, bit)
        return index

    def step_bit(h, t):
        return 1 + (h + t) % bits

    def remote(src, dst, send, recv, **device):
        return pltpu.make_async_remote_copy(
            src_ref=src, dst_ref=dst, send_sem=send, recv_sem=recv,
            device_id=device, device_id_type=MESH,
        )

    order = [0, 1, 3, 2] if n_grp >= 4 else [0, 1]
    order = order + list(range(len(order), n_grp))

    def take(i):
        return pltpu.make_async_copy(
            half_integrals.at[0, flip_grp(order[i])], taken.at[i % 2], taken_sem.at[i % 2]
        )

    take(0).start()
    barrier = pltpu.get_barrier_semaphore()
    for bit in range(bits + 1):
        pl.semaphore_signal(
            barrier, inc=1, device_id={"wide": flip(w, bit)}, device_id_type=MESH
        )
    for k in range(1, n_grp):
        pl.semaphore_signal(
            barrier, inc=1, device_id={"grp": flip_grp(k)}, device_id_type=MESH
        )

    owners = [plan[a, b] for a in range(plan.shape[0]) for b in range(plan.shape[1])]
    for last in range(slots - 1, 0, -1):
        for a in range(last):
            low = jnp.minimum(owners[a], owners[a + 1])
            owners[a + 1] = jnp.maximum(owners[a], owners[a + 1])
            owners[a] = low

    tile = 256 if virt % 256 == 0 else virt

    @pl.loop(0, virt // 128)
    def _(c):
        columns = pl.ds(pl.multiple_of(c * 128, 128), 128)
        coeff_t[columns, :] = coeff[:, columns].T

    def transform(i, rows_of):
        if i + 1 < n_grp:
            take(i + 1).start()
        take(i).wait()

        wide_tile = 256 if pb % 256 == 0 else pb

        @pl.loop(0, pb // wide_tile)
        def _(r):
            columns = pl.ds(pl.multiple_of(r * wide_tile, wide_tile), wide_tile)
            rows_of[:, columns] = jnp.dot(
                coeff_t[...], taken[i % 2, :, columns], preferred_element_type=jnp.float32
            ).astype(jnp.bfloat16)

    transform(0, mine.at[0])
    pl.semaphore_wait(barrier, bits + n_grp)

    sent = []

    def go(copy):
        copy.start()
        sent.append(copy)
        return copy

    middle = lax.rem(lax.div(g + 1, 2), 2) if n_grp >= 4 else 0

    def place(k):
        if n_grp < 4 or k % 4 < 2:
            return k
        return k + middle * (1 - 2 * (k % 2))

    def slice_of(k):
        if n_grp < 4 or k % 4 < 2:
            return flip_grp(k)
        return flip_grp(k) + middle * (flip_grp(k ^ 1) - flip_grp(k))

    a2a = [None]
    for k in range(1, n_grp):
        peer = flip_grp(k)
        a2a.append(remote(trans.at[k], mine.at[k], a2a_s.at[k], a2a_r.at[k], grp=peer))

    def second_sends():
        a2a[1].wait_send()
        if n_grp >= 4:
            pl.when(middle == 1)(a2a[3].wait_send)
            a2a[2].start()
        for k in range(4, n_grp):
            go(a2a[k])

    def third_sends():
        if n_grp >= 4:
            a2a[2].wait_send()

            a2a[3].start()

    near_in, msg_in, own_in = {}, {}, {}

    def start_near(k):
        at = place(k)
        if k:
            arrived = mine.at[at]
            pltpu.make_async_copy(arrived, arrived, a2a_r.at[at]).wait()
        if k == 2:
            pl.when(middle == 0)(third_sends)
        near_in[k] = go(remote(
            mine.at[at, pl.ds(sib_half, half)], sib.at[k], sib_s.at[k], sib_r.at[k], wide=flip(w, 0)
        ))
        for h in range(paths):
            peer = flip(w, step_bit(h, 0))
            rows = pl.ds(pl.multiple_of(my_half + h * rb, 16), rb)
            near_in[k, h, 0] = go(remote(
                mine.at[at, rows], near.at[k, h, 0], near_s.at[k, h, 0], near_r.at[k, h, 0], wide=peer
            ))

    def finish_near(k):
        near_in[k].wait_recv()
        for h in range(paths):
            peer = flip(w, step_bit(h, 0))
            near_in[k, h, 1] = go(remote(
                sib.at[k, pl.ds(h * rb, rb)], near.at[k, h, 1],
                near_s.at[k, h, 1], near_r.at[k, h, 1], wide=peer,
            ))

    def same(owner, index):
        return owner == index

    def in_far(owner, h, t):
        inside = [0] + [step_bit(h, u) for u in range(t)]
        there = flip(w, step_bit(h, t))
        ok = None
        for bit in range(bits + 1):
            if bit in inside:
                continue
            agree = lax.rem(lax.div(owner, 1 << bit), 2) == lax.rem(lax.div(there, 1 << bit), 2)
            ok = agree if ok is None else jnp.logical_and(ok, agree)
        return ok

    def pick(k, h, t, r, who, unit):
        rows = 32 if rb % 32 == 0 else 16
        at = pl.multiple_of(r * rows, rows)
        value = mine[place(k), pl.ds(pl.multiple_of(my_half + h * rb + at, 16), rows), :]
        first = flip(w, step_bit(h, 0))
        choices = [
            (flip(w, 0), lambda: sib[k, pl.ds(pl.multiple_of(h * rb + at, 16), rows), :]),
            (first, lambda: near[k, h, 0, pl.ds(at, rows), :]),
            (flip(first, 0), lambda: near[k, h, 1, pl.ds(at, rows), :]),
        ]
        for index, load in choices:
            for owner in who:
                value = lax.select(same(owner, index), load(), value)
        for u in range(1, t):
            for owner in who:
                value = lax.select(
                    in_far(owner, h, u), far[k, h, u - 1, unit, pl.ds(at, rows), :], value
                )
        return value

    def row_loop(body):
        rows = 32 if rb % 32 == 0 else 16

        @pl.loop(0, rb // rows)
        def _(r):
            body(r, pl.multiple_of(r * rows, rows), rows)

    def exchange_far(k, t):
        for h in range(paths):
            if t == 1:
                near_in[k, h, 0].wait_recv()
                near_in[k, h, 1].wait_recv()
            else:
                msg_in[k, h, t - 1].wait_recv()

            def body(r, at, rows):
                for unit in range(slots - 1):
                    who = [0, n_wide - 1] if unit == 0 else [owners[unit]]
                    msg[k, h, t - 1, unit, pl.ds(at, rows), :] = pick(k, h, t, r, who, unit)

            row_loop(body)
            msg_in[k, h, t] = go(remote(
                msg.at[k, h, t - 1], far.at[k, h, t - 1],
                msg_s.at[k, h, t - 1], msg_r.at[k, h, t - 1], wide=flip(w, step_bit(h, t)),
            ))

    def to_sibling(k):
        for h in range(paths):
            msg_in[k, h, bits - 1].wait_recv()

            def body(r, at, rows):
                for s in range(slots):
                    unit = 0 if s in (0, slots - 1) else s
                    who = {0: 0, slots - 1: n_wide - 1}.get(s)
                    who = owners[s] if who is None else who
                    owned[k, s, pl.ds(pl.multiple_of(my_half + h * rb + at, 16), rows), :] = pick(
                        k, h, bits, r, [who], unit
                    )

            row_loop(body)
        part = owned.at[k, :, pl.ds(my_half, half), :]
        own_in[k] = go(remote(part, part, own_s.at[k], own_r.at[k], wide=flip(w, 0)))

    contract = (((1,), (1,)), ((), ()))

    def intersect(k, lowest, highest):
        if lowest == 0:
            own_in[k].wait_recv()
            columns = pl.ds(pl.multiple_of(slice_of(k) * pb, 128), pb)
            outs.append(pltpu.make_async_copy(
                owned.at[k], owned_out.at[:, :, columns], owned_sem.at[k]
            ))
            outs[-1].start()

        @pl.loop(lowest, highest)
        def _(s):
            @pl.loop(0, virt // tile)
            def _(r):
                part = pl.ds(pl.multiple_of(r * tile, tile), tile)
                straight = lax.dot_general(
                    mine[place(k)], owned[k, s, part, :], contract,
                    preferred_element_type=jnp.float32,
                )
                turned = lax.dot_general(
                    owned[k, s], mine[place(k), part, :], contract,
                    preferred_element_type=jnp.float32,
                )
                value = 2.0 * straight - turned
                if k:
                    value = value + acc[s, :, part]
                acc[s, :, part] = value

    outs = []
    start_near(0)
    transform(1, trans.at[1])
    a2a[1].start()
    finish_near(0)
    for i in range(2, n_grp):
        transform(i, trans.at[order[i]])
        if order[i] == 3:
            pl.when(middle == 1)(a2a[3].start)

    @pl.loop(0, virt // 128)
    def _(c):
        part = pl.ds(pl.multiple_of(c * 128, 128), 128)
        vir_col[part, :] = jnp.broadcast_to(vir[part].reshape(1, 128), (128, 128)).T

    for t in range(1, bits):
        exchange_far(0, t)
    second_sends()
    cut = slots // 2
    for k in range(n_grp):
        last = k + 1 == n_grp
        if k:
            intersect(k - 1, 0, slots if last else cut)
        if not last:
            start_near(k + 1)
            finish_near(k + 1)
        to_sibling(k)
        if k and not last:
            intersect(k - 1, cut, slots)
        if not last:
            for t in range(1, bits):
                exchange_far(k + 1, t)
    intersect(n_grp - 1, 0, slots)

    for s in range(slots):
        total = occ[g, w] + occ[g, owners[s]]
        part = pl.ds(s * virt, virt)

        @pl.loop(0, virt // tile)
        def _(r):
            rows = pl.ds(pl.multiple_of(r * tile, tile), tile)
            denominator = (total - vir_col[rows, :1]) - vir[...].reshape(1, virt)
            comb[rows, part] = (acc[s, rows, :] / denominator).astype(jnp.bfloat16)

        outs.append(pltpu.make_async_copy(comb.at[:, part], comb_out.at[:, part], comb_sem.at[s]))
        outs[-1].start()
    for copy in outs:
        copy.wait()
    if n_grp >= 4:
        pl.when(middle == 1)(a2a[2].wait_send)
        pl.when(middle == 0)(a2a[3].wait_send)
    for copy in sent:
        copy.wait_send()


def shards(n_grp, n_wide, half_integrals, coeff_virtual, occ_energy, vir_energy, plan):
    basis, virt = coeff_virtual.shape
    pb = half_integrals.shape[3]
    slots = plan.size
    bits = n_wide.bit_length() - 2
    paths = bits if virt % (32 * bits) == 0 else 1
    rb = virt // 2 // paths
    bf16, f32 = jnp.bfloat16, jnp.float32
    dma = pltpu.SemaphoreType.DMA
    smem = pl.BlockSpec(memory_space=pltpu.SMEM)
    vmem = pl.BlockSpec(memory_space=pltpu.VMEM)
    hbm = pl.BlockSpec(memory_space=pl.ANY)
    flops = 2 * 2 * slots * virt * virt * pb * n_grp
    comb, owned = pl.pallas_call(
        functools.partial(kernel, n_grp, n_wide, slots, paths),
        out_shape=[
            jax.ShapeDtypeStruct((virt, slots * virt), bf16),
            jax.ShapeDtypeStruct((slots, virt, n_grp * pb), bf16),
        ],
        in_specs=[smem, smem, vmem, vmem, hbm],
        out_specs=[hbm, hbm],
        scratch_shapes=[
            pltpu.VMEM((n_grp, virt, pb), bf16),
            pltpu.VMEM((n_grp, virt // 2, pb), bf16),
            pltpu.VMEM((n_grp, paths, 2, rb, pb), bf16),
            pltpu.VMEM((n_grp, paths, bits - 1, slots - 1, rb, pb), bf16),
            pltpu.VMEM((n_grp, paths, bits - 1, slots - 1, rb, pb), bf16),
            pltpu.VMEM((n_grp, slots, virt, pb), bf16),
            pltpu.VMEM((slots, virt, virt), f32),
            pltpu.VMEM((virt, slots * virt), bf16),
            pltpu.VMEM((n_grp, virt, pb), bf16),
            pltpu.VMEM((2, basis, pb), bf16),
            pltpu.VMEM((virt, basis), bf16),
            pltpu.VMEM((virt, 128), f32),
            dma((2,)),
            dma((n_grp,)), dma((n_grp,)),
            dma((n_grp,)), dma((n_grp,)),
            dma((n_grp, paths, 2)), dma((n_grp, paths, 2)),
            dma((n_grp, paths, bits - 1)), dma((n_grp, paths, bits - 1)),
            dma((n_grp,)), dma((n_grp,)),
            dma((n_grp,)), dma((slots,)),
        ],
        compiler_params=pltpu.CompilerParams(
            collective_id=0, has_side_effects=True, vmem_limit_bytes=63 * 1024 * 1024
        ),
        cost_estimate=pl.CostEstimate(
            flops=flops, bytes_accessed=16 * virt * pb * n_grp, transcendentals=0
        ),
    )(plan, occ_energy.T, vir_energy, coeff_virtual, half_integrals)
    density = jnp.dot(
        comb, owned.reshape(slots * virt, n_grp * pb), preferred_element_type=jnp.float32
    )
    return density[None, None]


def solution(mesh):
    return jax.shard_map(
        functools.partial(shards, mesh.shape["grp"], mesh.shape["wide"]),
        mesh=mesh,
        in_specs=(P("wide", None, None, "grp"), P(), P(), P(), P()),
        out_specs=P("wide", "grp", None, None),
        check_vma=False,
    )
```

```python
import functools

import jax
import jax.numpy as jnp
from jax import lax
from jax.experimental import pallas as pl
from jax.experimental.pallas import tpu as pltpu
from jax.sharding import PartitionSpec as P

MESH = pl.DeviceIdType.MESH


def kernel(
    n_grp, n_wide, slots, paths, n_sub,
    plan, occ, vir, coeff, half_integrals,
    comb_out, owned_out,
    mine, sib, near, msg, far, owned, acc, comb, trans, taken, coeff_t, vir_col,
    taken_sem, a2a_s, a2a_r, sib_s, sib_r, near_s, near_r, msg_s, msg_r, own_s, own_r, owned_sem, comb_sem,
):
    g = lax.axis_index("grp")
    w = lax.axis_index("wide")
    virt, pb = mine.shape[1], mine.shape[2]
    n_parts = n_grp * n_sub
    half = virt // 2
    rb = half // paths
    bits = n_wide.bit_length() - 2
    core = lax.rem(w, 2)
    my_half = pl.multiple_of(core * half, 16)
    sib_half = pl.multiple_of((1 - core) * half, 16)

    def flip(index, bit):
        size = 1 << bit
        return index + size - 2 * size * lax.rem(lax.div(index, size), 2)

    def flip_grp(k):
        index = g
        for bit in range(n_grp.bit_length() - 1):
            if (k >> bit) & 1:
                index = flip(index, bit)
        return index

    def step_bit(h, t):
        return 1 + (h + t) % bits

    def remote(src, dst, send, recv, **device):
        return pltpu.make_async_remote_copy(
            src_ref=src, dst_ref=dst, send_sem=send, recv_sem=recv,
            device_id=device, device_id_type=MESH,
        )

    order = [0, 1, 3, 2] if n_grp >= 4 else [0, 1]
    order = order + list(range(len(order), n_grp))

    def take(i):
        return pltpu.make_async_copy(
            half_integrals.at[0, flip_grp(order[i])], taken.at[i % 2], taken_sem.at[i % 2]
        )

    take(0).start()
    barrier = pltpu.get_barrier_semaphore()
    for bit in range(bits + 1):
        pl.semaphore_signal(
            barrier, inc=1, device_id={"wide": flip(w, bit)}, device_id_type=MESH
        )
    for k in range(1, n_grp):
        pl.semaphore_signal(
            barrier, inc=1, device_id={"grp": flip_grp(k)}, device_id_type=MESH
        )

    owners = [plan[a, b] for a in range(plan.shape[0]) for b in range(plan.shape[1])]
    for last in range(slots - 1, 0, -1):
        for a in range(last):
            low = jnp.minimum(owners[a], owners[a + 1])
            owners[a + 1] = jnp.maximum(owners[a], owners[a + 1])
            owners[a] = low

    tile = 256 if virt % 256 == 0 else virt

    @pl.loop(0, virt // 128)
    def _(c):
        columns = pl.ds(pl.multiple_of(c * 128, 128), 128)
        coeff_t[columns, :] = coeff[:, columns].T

    def transform(i, rows_of):
        if i + 1 < n_grp:
            take(i + 1).start()
        take(i).wait()

        for c in range(n_sub):
            rows_of[order[i] * n_sub + c] = jnp.dot(
                coeff_t[...], taken[i % 2, :, c * pb:(c + 1) * pb],
                preferred_element_type=jnp.float32,
            ).astype(jnp.bfloat16)

    transform(0, mine)
    pl.semaphore_wait(barrier, bits + n_grp)

    sent = []

    def go(copy):
        copy.start()
        sent.append(copy)
        return copy

    middle = lax.rem(lax.div(g + 1, 2), 2) if n_grp >= 4 else 0

    def place(j):
        if n_grp < 4 or j // n_sub % 4 < 2:
            return j
        return j + middle * n_sub * (1 - 2 * (j // n_sub % 2))

    def column_of(j):
        k = j // n_sub
        if n_grp < 4 or k % 4 < 2:
            index = flip_grp(k)
        else:
            index = flip_grp(k) + middle * (flip_grp(k ^ 1) - flip_grp(k))
        return pl.multiple_of(index * (n_sub * pb) + j % n_sub * pb, 128)

    def a2a(k):
        for j in range(k * n_sub, (k + 1) * n_sub):
            yield remote(trans.at[j], mine.at[j], a2a_s.at[j], a2a_r.at[j], grp=flip_grp(k))

    def send(k):
        for copy in a2a(k):
            copy.start()

    def wait_sent(k):
        for copy in a2a(k):
            copy.wait_send()

    def second_sends():
        wait_sent(1)
        if n_grp >= 4:
            pl.when(middle == 1)(lambda: wait_sent(3))
            send(2)
        for k in range(4, n_grp):
            send(k)

    def third_sends():
        wait_sent(2)
        send(3)

    near_in, msg_in, own_in = {}, {}, {}

    def start_near(k):
        at = place(k)
        if k >= n_sub:
            arrived = mine.at[at]
            pltpu.make_async_copy(arrived, arrived, a2a_r.at[at]).wait()
        if n_grp >= 4 and k == 3 * n_sub - 1:
            pl.when(middle == 0)(third_sends)
        near_in[k] = go(remote(
            mine.at[at, pl.ds(sib_half, half)], sib.at[k], sib_s.at[k], sib_r.at[k], wide=flip(w, 0)
        ))
        for h in range(paths):
            peer = flip(w, step_bit(h, 0))
            rows = pl.ds(pl.multiple_of(my_half + h * rb, 16), rb)
            near_in[k, h, 0] = go(remote(
                mine.at[at, rows], near.at[k, h, 0], near_s.at[k, h, 0], near_r.at[k, h, 0], wide=peer
            ))

    def finish_near(k):
        near_in[k].wait_recv()
        for h in range(paths):
            peer = flip(w, step_bit(h, 0))
            near_in[k, h, 1] = go(remote(
                sib.at[k, pl.ds(h * rb, rb)], near.at[k, h, 1],
                near_s.at[k, h, 1], near_r.at[k, h, 1], wide=peer,
            ))

    def same(owner, index):
        return owner == index

    def in_far(owner, h, t):
        inside = [0] + [step_bit(h, u) for u in range(t)]
        there = flip(w, step_bit(h, t))
        ok = None
        for bit in range(bits + 1):
            if bit in inside:
                continue
            agree = lax.rem(lax.div(owner, 1 << bit), 2) == lax.rem(lax.div(there, 1 << bit), 2)
            ok = agree if ok is None else jnp.logical_and(ok, agree)
        return ok

    def pick(k, h, t, r, who, unit):
        rows = 32 if rb % 32 == 0 else 16
        at = pl.multiple_of(r * rows, rows)
        value = mine[place(k), pl.ds(pl.multiple_of(my_half + h * rb + at, 16), rows), :]
        first = flip(w, step_bit(h, 0))
        choices = [
            (flip(w, 0), lambda: sib[k, pl.ds(pl.multiple_of(h * rb + at, 16), rows), :]),
            (first, lambda: near[k, h, 0, pl.ds(at, rows), :]),
            (flip(first, 0), lambda: near[k, h, 1, pl.ds(at, rows), :]),
        ]
        for index, load in choices:
            for owner in who:
                value = lax.select(same(owner, index), load(), value)
        for u in range(1, t):
            for owner in who:
                value = lax.select(
                    in_far(owner, h, u), far[k, h, u - 1, unit, pl.ds(at, rows), :], value
                )
        return value

    def row_loop(body):
        rows = 32 if rb % 32 == 0 else 16

        @pl.loop(0, rb // rows)
        def _(r):
            body(r, pl.multiple_of(r * rows, rows), rows)

    def exchange_far(k, t):
        for h in range(paths):
            if t == 1:
                near_in[k, h, 0].wait_recv()
                near_in[k, h, 1].wait_recv()
            else:
                msg_in[k, h, t - 1].wait_recv()

            def body(r, at, rows):
                for unit in range(slots - 1):
                    who = [0, n_wide - 1] if unit == 0 else [owners[unit]]
                    msg[k, h, t - 1, unit, pl.ds(at, rows), :] = pick(k, h, t, r, who, unit)

            row_loop(body)
            msg_in[k, h, t] = go(remote(
                msg.at[k, h, t - 1], far.at[k, h, t - 1],
                msg_s.at[k, h, t - 1], msg_r.at[k, h, t - 1], wide=flip(w, step_bit(h, t)),
            ))

    def to_sibling(k):
        for h in range(paths):
            msg_in[k, h, bits - 1].wait_recv()

            def body(r, at, rows):
                for s in range(slots):
                    unit = 0 if s in (0, slots - 1) else s
                    who = {0: 0, slots - 1: n_wide - 1}.get(s)
                    who = owners[s] if who is None else who
                    owned[k, s, pl.ds(pl.multiple_of(my_half + h * rb + at, 16), rows), :] = pick(
                        k, h, bits, r, [who], unit
                    )

            row_loop(body)
        part = owned.at[k, :, pl.ds(my_half, half), :]
        own_in[k] = go(remote(part, part, own_s.at[k], own_r.at[k], wide=flip(w, 0)))

    contract = (((1,), (1,)), ((), ()))

    def store_rows(k):
        own_in[k].wait_recv()
        outs.append(pltpu.make_async_copy(
            owned.at[k], owned_out.at[:, :, pl.ds(column_of(k), pb)], owned_sem.at[k]
        ))
        outs[-1].start()

    def intersect(parts, lowest, highest):
        @pl.loop(lowest, highest)
        def _(s):
            @pl.loop(0, virt // tile)
            def _(r):
                part = pl.ds(pl.multiple_of(r * tile, tile), tile)
                value = None if parts[0] == 0 else acc[s, :, part]
                for j in parts:
                    straight = lax.dot_general(
                        mine[place(j)], owned[j, s, part, :], contract,
                        preferred_element_type=jnp.float32,
                    )
                    turned = lax.dot_general(
                        owned[j, s], mine[place(j), part, :], contract,
                        preferred_element_type=jnp.float32,
                    )
                    term = 2.0 * straight - turned
                    value = term if value is None else value + term
                acc[s, :, part] = value

    outs = []
    start_near(0)
    transform(1, trans)
    send(1)
    finish_near(0)
    for i in range(2, n_grp):
        transform(i, trans)
        if order[i] == 3:
            pl.when(middle == 1)(lambda: send(3))

    @pl.loop(0, virt // 128)
    def _(c):
        part = pl.ds(pl.multiple_of(c * 128, 128), 128)
        vir_col[part, :] = jnp.broadcast_to(vir[part].reshape(1, 128), (128, 128)).T

    cut = slots // 2
    todo = []
    for j in range(n_parts):
        if j + 1 < n_parts:
            if j + 1 == 2 * n_sub - 1:
                second_sends()
            start_near(j + 1)
            finish_near(j + 1)
        for t in range(1, bits):
            exchange_far(j, t)
        if j:
            to_sibling(j - 1)
        if j >= 2:
            store_rows(j - 2)
            if (j - 1) % n_sub == 0:
                parts = list(range(j - 1 - n_sub, j - 1))
                todo += [(parts, 0, cut), (parts, cut, slots)]
        for _ in range(2 // n_sub):
            if todo:
                intersect(*todo.pop(0))
    for item in todo:
        intersect(*item)
    to_sibling(n_parts - 1)
    if n_parts >= 2:
        store_rows(n_parts - 2)
        if n_sub > 1:
            intersect(list(range(n_parts - n_sub, n_parts - 1)), 0, slots)
        else:
            intersect([n_parts - 2], 0, slots)
    store_rows(n_parts - 1)
    intersect([n_parts - 1], 0, slots)

    for s in range(slots):
        total = occ[g, w] + occ[g, owners[s]]
        part = pl.ds(s * virt, virt)

        @pl.loop(0, virt // tile)
        def _(r):
            rows = pl.ds(pl.multiple_of(r * tile, tile), tile)
            denominator = (total - vir_col[rows, :1]) - vir[...].reshape(1, virt)
            comb[rows, part] = (acc[s, rows, :] / denominator).astype(jnp.bfloat16)

        outs.append(pltpu.make_async_copy(comb.at[:, part], comb_out.at[:, part], comb_sem.at[s]))
        outs[-1].start()
    for copy in outs:
        copy.wait()
    if n_grp >= 4:
        pl.when(middle == 1)(lambda: wait_sent(2))
        pl.when(middle == 0)(lambda: wait_sent(3))
    for k in range(4, n_grp):
        wait_sent(k)
    for copy in sent:
        copy.wait_send()


def shards(n_grp, n_wide, half_integrals, coeff_virtual, occ_energy, vir_energy, plan):
    basis, virt = coeff_virtual.shape
    aux = half_integrals.shape[3]
    n_sub = 2 if aux % 512 == 0 else 1
    pb = aux // n_sub
    n_parts = n_grp * n_sub
    slots = plan.size
    bits = n_wide.bit_length() - 2
    paths = bits if virt % (32 * bits) == 0 else 1
    rb = virt // 2 // paths
    bf16, f32 = jnp.bfloat16, jnp.float32
    dma = pltpu.SemaphoreType.DMA
    smem = pl.BlockSpec(memory_space=pltpu.SMEM)
    vmem = pl.BlockSpec(memory_space=pltpu.VMEM)
    hbm = pl.BlockSpec(memory_space=pl.ANY)
    flops = 2 * 2 * slots * virt * virt * aux * n_grp
    comb, owned = pl.pallas_call(
        functools.partial(kernel, n_grp, n_wide, slots, paths, n_sub),
        out_shape=[
            jax.ShapeDtypeStruct((virt, slots * virt), bf16),
            jax.ShapeDtypeStruct((slots, virt, n_grp * aux), bf16),
        ],
        in_specs=[smem, smem, vmem, vmem, hbm],
        out_specs=[hbm, hbm],
        scratch_shapes=[
            pltpu.VMEM((n_parts, virt, pb), bf16),
            pltpu.VMEM((n_parts, virt // 2, pb), bf16),
            pltpu.VMEM((n_parts, paths, 2, rb, pb), bf16),
            pltpu.VMEM((n_parts, paths, bits - 1, slots - 1, rb, pb), bf16),
            pltpu.VMEM((n_parts, paths, bits - 1, slots - 1, rb, pb), bf16),
            pltpu.VMEM((n_parts, slots, virt, pb), bf16),
            pltpu.VMEM((slots, virt, virt), f32),
            pltpu.VMEM((virt, slots * virt), bf16),
            pltpu.VMEM((n_parts, virt, pb), bf16),
            pltpu.VMEM((2, basis, aux), bf16),
            pltpu.VMEM((virt, basis), bf16),
            pltpu.VMEM((virt, 128), f32),
            dma((2,)),
            dma((n_parts,)), dma((n_parts,)),
            dma((n_parts,)), dma((n_parts,)),
            dma((n_parts, paths, 2)), dma((n_parts, paths, 2)),
            dma((n_parts, paths, bits - 1)), dma((n_parts, paths, bits - 1)),
            dma((n_parts,)), dma((n_parts,)),
            dma((n_parts,)), dma((slots,)),
        ],
        compiler_params=pltpu.CompilerParams(
            collective_id=0, has_side_effects=True, vmem_limit_bytes=63 * 1024 * 1024
        ),
        cost_estimate=pl.CostEstimate(
            flops=flops, bytes_accessed=16 * virt * aux * n_grp, transcendentals=0
        ),
    )(plan, occ_energy.T, vir_energy, coeff_virtual, half_integrals)
    density = jnp.dot(
        comb, owned.reshape(slots * virt, n_grp * aux), preferred_element_type=jnp.float32
    )
    return density[None, None]


def solution(mesh):
    return jax.shard_map(
        functools.partial(shards, mesh.shape["grp"], mesh.shape["wide"]),
        mesh=mesh,
        in_specs=(P("wide", None, None, "grp"), P(), P(), P(), P()),
        out_specs=P("wide", "grp", None, None),
        check_vma=False,
    )
```

```python
import functools

import jax
import jax.numpy as jnp
from jax import lax
from jax.experimental import pallas as pl
from jax.experimental.pallas import tpu as pltpu
from jax.sharding import PartitionSpec as P

MESH = pl.DeviceIdType.MESH


def kernel(
    n_grp, n_wide, slots, paths, n_sub,
    plan, occ, vir, coeff, half_integrals,
    comb_out, owned_out,
    mine, sib, near, msg, far, owned, acc, comb, trans, taken, coeff_t, vir_col, vir_row,
    taken_sem, a2a_s, a2a_r, sib_s, sib_r, near_s, near_r, msg_s, msg_r, own_s, own_r, owned_sem, comb_sem,
):
    g = lax.axis_index("grp")
    w = lax.axis_index("wide")
    virt, pb = mine.shape[1], mine.shape[2]
    n_parts = n_grp * n_sub
    half = virt // 2
    rb = half // paths
    bits = n_wide.bit_length() - 2
    core = lax.rem(w, 2)
    my_half = pl.multiple_of(core * half, 16)
    sib_half = pl.multiple_of((1 - core) * half, 16)

    def flip(index, bit):
        size = 1 << bit
        return index + size - 2 * size * lax.rem(lax.div(index, size), 2)

    def flip_grp(k):
        index = g
        for bit in range(n_grp.bit_length() - 1):
            if (k >> bit) & 1:
                index = flip(index, bit)
        return index

    def step_bit(h, t):
        return 1 + (h + t) % bits

    def remote(src, dst, send, recv, **device):
        return pltpu.make_async_remote_copy(
            src_ref=src, dst_ref=dst, send_sem=send, recv_sem=recv,
            device_id=device, device_id_type=MESH,
        )

    order = [0, 1, 3, 2] if n_grp >= 4 else [0, 1]
    order = order + list(range(len(order), n_grp))

    def take(i):
        return pltpu.make_async_copy(
            half_integrals.at[0, flip_grp(order[i])], taken.at[i % 2], taken_sem.at[i % 2]
        )

    take(0).start()
    barrier = pltpu.get_barrier_semaphore()
    for bit in range(bits + 1):
        pl.semaphore_signal(
            barrier, inc=1, device_id={"wide": flip(w, bit)}, device_id_type=MESH
        )
    for k in range(1, n_grp):
        pl.semaphore_signal(
            barrier, inc=1, device_id={"grp": flip_grp(k)}, device_id_type=MESH
        )

    owners = [plan[a, b] for a in range(plan.shape[0]) for b in range(plan.shape[1])]
    for last in range(slots - 1, 0, -1):
        for a in range(last):
            low = jnp.minimum(owners[a], owners[a + 1])
            owners[a + 1] = jnp.maximum(owners[a], owners[a + 1])
            owners[a] = low

    tile = 256 if virt % 256 == 0 else virt

    @pl.loop(0, virt // 128)
    def _(c):
        columns = pl.ds(pl.multiple_of(c * 128, 128), 128)
        coeff_t[columns, :] = coeff[:, columns].T

    def transform(i, rows_of):
        if i + 1 < n_grp:
            take(i + 1).start()
        take(i).wait()

        for c in range(n_sub):
            rows_of[order[i] * n_sub + c] = jnp.dot(
                coeff_t[...], taken[i % 2, :, c * pb:(c + 1) * pb],
                preferred_element_type=jnp.float32,
            ).astype(jnp.bfloat16)

    transform(0, mine)
    pl.semaphore_wait(barrier, bits + n_grp)

    sent = []

    def go(copy):
        copy.start()
        sent.append(copy)
        return copy

    middle = lax.rem(lax.div(g + 1, 2), 2) if n_grp >= 4 else 0

    def place(j):
        if n_grp < 4 or j // n_sub % 4 < 2:
            return j
        return j + middle * n_sub * (1 - 2 * (j // n_sub % 2))

    def column_of(j):
        k = j // n_sub
        if n_grp < 4 or k % 4 < 2:
            index = flip_grp(k)
        else:
            index = flip_grp(k) + middle * (flip_grp(k ^ 1) - flip_grp(k))
        return pl.multiple_of(index * (n_sub * pb) + j % n_sub * pb, 128)

    def a2a(k):
        for j in range(k * n_sub, (k + 1) * n_sub):
            yield remote(trans.at[j], mine.at[j], a2a_s.at[j], a2a_r.at[j], grp=flip_grp(k))

    def send(k):
        for copy in a2a(k):
            copy.start()

    def wait_sent(k):
        for copy in a2a(k):
            copy.wait_send()

    def second_sends():
        wait_sent(1)
        if n_grp >= 4:
            pl.when(middle == 1)(lambda: wait_sent(3))
            send(2)
        for k in range(4, n_grp):
            send(k)

    def third_sends():
        wait_sent(2)
        send(3)

    near_in, msg_in, own_in = {}, {}, {}

    def start_near(k):
        at = place(k)
        if k >= n_sub:
            arrived = mine.at[at]
            pltpu.make_async_copy(arrived, arrived, a2a_r.at[at]).wait()
        if n_grp >= 4 and k == 3 * n_sub - 1:
            pl.when(middle == 0)(third_sends)
        near_in[k] = go(remote(
            mine.at[at, pl.ds(sib_half, half)], sib.at[k], sib_s.at[k], sib_r.at[k], wide=flip(w, 0)
        ))
        for h in range(paths):
            peer = flip(w, step_bit(h, 0))
            rows = pl.ds(pl.multiple_of(my_half + h * rb, 16), rb)
            near_in[k, h, 0] = go(remote(
                mine.at[at, rows], near.at[k, h, 0], near_s.at[k, h, 0], near_r.at[k, h, 0], wide=peer
            ))

    def finish_near(k):
        near_in[k].wait_recv()
        for h in range(paths):
            peer = flip(w, step_bit(h, 0))
            near_in[k, h, 1] = go(remote(
                sib.at[k, pl.ds(h * rb, rb)], near.at[k, h, 1],
                near_s.at[k, h, 1], near_r.at[k, h, 1], wide=peer,
            ))

    def same(owner, index):
        return owner == index

    def in_far(owner, h, t):
        inside = [0] + [step_bit(h, u) for u in range(t)]
        there = flip(w, step_bit(h, t))
        ok = None
        for bit in range(bits + 1):
            if bit in inside:
                continue
            agree = lax.rem(lax.div(owner, 1 << bit), 2) == lax.rem(lax.div(there, 1 << bit), 2)
            ok = agree if ok is None else jnp.logical_and(ok, agree)
        return ok

    def pick(k, h, t, r, who, unit):
        rows = 32 if rb % 32 == 0 else 16
        at = pl.multiple_of(r * rows, rows)
        value = mine[place(k), pl.ds(pl.multiple_of(my_half + h * rb + at, 16), rows), :]
        first = flip(w, step_bit(h, 0))
        choices = [
            (flip(w, 0), lambda: sib[k, pl.ds(pl.multiple_of(h * rb + at, 16), rows), :]),
            (first, lambda: near[k, h, 0, pl.ds(at, rows), :]),
            (flip(first, 0), lambda: near[k, h, 1, pl.ds(at, rows), :]),
        ]
        for index, load in choices:
            for owner in who:
                value = lax.select(same(owner, index), load(), value)
        for u in range(1, t):
            for owner in who:
                value = lax.select(
                    in_far(owner, h, u), far[k, h, u - 1, unit, pl.ds(at, rows), :], value
                )
        return value

    def row_loop(body):
        rows = 32 if rb % 32 == 0 else 16

        @pl.loop(0, rb // rows)
        def _(r):
            body(r, pl.multiple_of(r * rows, rows), rows)

    def exchange_far(k, t):
        for h in range(paths):
            if t == 1:
                near_in[k, h, 0].wait_recv()
                near_in[k, h, 1].wait_recv()
            else:
                msg_in[k, h, t - 1].wait_recv()

            def body(r, at, rows):
                for unit in range(slots - 1):
                    who = [0, n_wide - 1] if unit == 0 else [owners[unit]]
                    msg[k, h, t - 1, unit, pl.ds(at, rows), :] = pick(k, h, t, r, who, unit)

            row_loop(body)
            msg_in[k, h, t] = go(remote(
                msg.at[k, h, t - 1], far.at[k, h, t - 1],
                msg_s.at[k, h, t - 1], msg_r.at[k, h, t - 1], wide=flip(w, step_bit(h, t)),
            ))

    def to_sibling(k):
        for h in range(paths):
            msg_in[k, h, bits - 1].wait_recv()

            def body(r, at, rows):
                for s in range(slots):
                    unit = 0 if s in (0, slots - 1) else s
                    who = {0: 0, slots - 1: n_wide - 1}.get(s)
                    who = owners[s] if who is None else who
                    owned[k, s, pl.ds(pl.multiple_of(my_half + h * rb + at, 16), rows), :] = pick(
                        k, h, bits, r, [who], unit
                    )

            row_loop(body)
        part = owned.at[k, :, pl.ds(my_half, half), :]
        own_in[k] = go(remote(part, part, own_s.at[k], own_r.at[k], wide=flip(w, 0)))

    contract = (((1,), (1,)), ((), ()))

    def store_rows(k):
        own_in[k].wait_recv()
        outs.append(pltpu.make_async_copy(
            owned.at[k], owned_out.at[:, :, pl.ds(column_of(k), pb)], owned_sem.at[k]
        ))
        outs[-1].start()

    def term_of(j, s, part):
        straight = lax.dot_general(
            mine[place(j)], owned[j, s, part, :], contract, preferred_element_type=jnp.float32
        )
        turned = lax.dot_general(
            owned[j, s], mine[place(j), part, :], contract, preferred_element_type=jnp.float32
        )
        return 2.0 * straight - turned

    def intersect(parts, lowest, highest):
        @pl.loop(lowest, highest)
        def _(s):
            @pl.loop(0, virt // tile)
            def _(r):
                part = pl.ds(pl.multiple_of(r * tile, tile), tile)
                value = None if parts[0] == 0 else acc[s, :, part]
                for j in parts:
                    term = term_of(j, s, part)
                    value = term if value is None else value + term
                acc[s, :, part] = value

    outs = []
    start_near(0)
    transform(1, trans)
    send(1)
    finish_near(0)
    for i in range(2, n_grp):
        transform(i, trans)
        if order[i] == 3:
            pl.when(middle == 1)(lambda: send(3))

    @pl.loop(0, virt // 128)
    def _(c):
        part = pl.ds(pl.multiple_of(c * 128, 128), 128)
        vir_row[:, part] = vir[part].reshape(1, 128)
        vir_col[part, :] = jnp.broadcast_to(vir[part].reshape(1, 128), (128, 128)).T

    cut = slots // 2
    todo = []
    for j in range(n_parts):
        if j + 1 < n_parts:
            if j + 1 == 2 * n_sub - 1:
                second_sends()
            start_near(j + 1)
            finish_near(j + 1)
        for t in range(1, bits):
            exchange_far(j, t)
        if j:
            to_sibling(j - 1)
        if j >= 2:
            store_rows(j - 2)
            if (j - 1) % n_sub == 0:
                parts = list(range(j - 1 - n_sub, j - 1))
                todo += [(parts, 0, cut), (parts, cut, slots)]
        for _ in range(2 // n_sub):
            if todo:
                intersect(*todo.pop(0))
    for item in todo:
        intersect(*item)
    to_sibling(n_parts - 1)
    if n_parts >= 2:
        store_rows(n_parts - 2)
        if n_sub > 1:
            intersect(list(range(n_parts - n_sub, n_parts - 1)), 0, slots)
        else:
            intersect([n_parts - 2], 0, slots)
    store_rows(n_parts - 1)

    for s in range(slots):
        total = occ[g, w] + occ[g, owners[s]]

        @pl.loop(0, virt // tile)
        def _(r):
            part = pl.ds(pl.multiple_of(r * tile, tile), tile)
            value = acc[s, :, part] + term_of(n_parts - 1, s, part)
            denominator = (total - vir_col[:, :1]) - vir_row[:, part]
            comb[:, pl.ds(pl.multiple_of(s * virt + r * tile, tile), tile)] = (
                value / denominator
            ).astype(jnp.bfloat16)

        part = pl.ds(s * virt, virt)
        outs.append(pltpu.make_async_copy(comb.at[:, part], comb_out.at[:, part], comb_sem.at[s]))
        outs[-1].start()
    for copy in outs:
        copy.wait()
    if n_grp >= 4:
        pl.when(middle == 1)(lambda: wait_sent(2))
        pl.when(middle == 0)(lambda: wait_sent(3))
    for k in range(4, n_grp):
        wait_sent(k)
    for copy in sent:
        copy.wait_send()


def density_kernel(comb, owned, out):
    slots, virt, columns = owned.shape
    out[...] = jnp.dot(
        comb[...], owned[...].reshape(slots * virt, columns), preferred_element_type=jnp.float32
    )


def shards(n_grp, n_wide, half_integrals, coeff_virtual, occ_energy, vir_energy, plan):
    basis, virt = coeff_virtual.shape
    aux = half_integrals.shape[3]
    n_sub = 2 if aux % 512 == 0 else 1
    pb = aux // n_sub
    n_parts = n_grp * n_sub
    slots = plan.size
    bits = n_wide.bit_length() - 2
    paths = bits if virt % (32 * bits) == 0 else 1
    rb = virt // 2 // paths
    bf16, f32 = jnp.bfloat16, jnp.float32
    dma = pltpu.SemaphoreType.DMA
    smem = pl.BlockSpec(memory_space=pltpu.SMEM)
    vmem = pl.BlockSpec(memory_space=pltpu.VMEM)
    hbm = pl.BlockSpec(memory_space=pl.ANY)
    flops = 2 * 2 * slots * virt * virt * aux * n_grp
    comb, owned = pl.pallas_call(
        functools.partial(kernel, n_grp, n_wide, slots, paths, n_sub),
        out_shape=[
            jax.ShapeDtypeStruct((virt, slots * virt), bf16),
            jax.ShapeDtypeStruct((slots, virt, n_grp * aux), bf16),
        ],
        in_specs=[smem, smem, vmem, vmem, hbm],
        out_specs=[hbm, hbm],
        scratch_shapes=[
            pltpu.VMEM((n_parts, virt, pb), bf16),
            pltpu.VMEM((n_parts, virt // 2, pb), bf16),
            pltpu.VMEM((n_parts, paths, 2, rb, pb), bf16),
            pltpu.VMEM((n_parts, paths, bits - 1, slots - 1, rb, pb), bf16),
            pltpu.VMEM((n_parts, paths, bits - 1, slots - 1, rb, pb), bf16),
            pltpu.VMEM((n_parts, slots, virt, pb), bf16),
            pltpu.VMEM((slots, virt, virt), f32),
            pltpu.VMEM((virt, slots * virt), bf16),
            pltpu.VMEM((n_parts, virt, pb), bf16),
            pltpu.VMEM((2, basis, aux), bf16),
            pltpu.VMEM((virt, basis), bf16),
            pltpu.VMEM((virt, 128), f32),
            pltpu.VMEM((1, virt), f32),
            dma((2,)),
            dma((n_parts,)), dma((n_parts,)),
            dma((n_parts,)), dma((n_parts,)),
            dma((n_parts, paths, 2)), dma((n_parts, paths, 2)),
            dma((n_parts, paths, bits - 1)), dma((n_parts, paths, bits - 1)),
            dma((n_parts,)), dma((n_parts,)),
            dma((n_parts,)), dma((slots,)),
        ],
        compiler_params=pltpu.CompilerParams(
            collective_id=0, has_side_effects=True, vmem_limit_bytes=63 * 1024 * 1024
        ),
        cost_estimate=pl.CostEstimate(
            flops=flops, bytes_accessed=16 * virt * aux * n_grp, transcendentals=0
        ),
    )(plan, occ_energy.T, vir_energy, coeff_virtual, half_integrals)
    span = n_grp * aux
    wide_tile = 256 if span % 256 == 0 else span
    density = pl.pallas_call(
        density_kernel,
        out_shape=jax.ShapeDtypeStruct((virt, span), f32),
        grid=(span // wide_tile,),
        in_specs=[
            pl.BlockSpec((virt, slots * virt), lambda c: (0, 0)),
            pl.BlockSpec((slots, virt, wide_tile), lambda c: (0, 0, c)),
        ],
        out_specs=pl.BlockSpec((virt, wide_tile), lambda c: (0, c)),
        compiler_params=pltpu.CompilerParams(vmem_limit_bytes=48 * 1024 * 1024),
        cost_estimate=pl.CostEstimate(
            flops=2 * slots * virt * virt * span, bytes_accessed=14 * virt * span,
            transcendentals=0,
        ),
    )(comb, owned)
    return density[None, None]


def solution(mesh):
    return jax.shard_map(
        functools.partial(shards, mesh.shape["grp"], mesh.shape["wide"]),
        mesh=mesh,
        in_specs=(P("wide", None, None, "grp"), P(), P(), P(), P()),
        out_specs=P("wide", "grp", None, None),
        check_vma=False,
    )
```

```python
import functools

import jax
import jax.numpy as jnp
from jax import lax
from jax.experimental import pallas as pl
from jax.experimental.pallas import tpu as pltpu
from jax.sharding import PartitionSpec as P

MESH = pl.DeviceIdType.MESH


def kernel(
    n_grp, n_wide, slots, paths, n_sub,
    plan, occ, vir, coeff, half_integrals,
    comb_out, owned_out,
    mine, sib, near, msg, far, owned, acc, comb, trans, taken, coeff_t, vir_col, vir_row,
    taken_sem, a2a_s, a2a_r, sib_s, sib_r, near_s, near_r, msg_s, msg_r, own_s, own_r, owned_sem, comb_sem,
):
    g = lax.axis_index("grp")
    w = lax.axis_index("wide")
    virt, pb = mine.shape[1], mine.shape[2]
    n_parts = n_grp * n_sub
    half = virt // 2
    rb = half // paths
    bits = n_wide.bit_length() - 2
    core = lax.rem(w, 2)
    my_half = pl.multiple_of(core * half, 16)
    sib_half = pl.multiple_of((1 - core) * half, 16)

    def flip(index, bit):
        size = 1 << bit
        return index + size - 2 * size * lax.rem(lax.div(index, size), 2)

    def flip_grp(k):
        index = g
        for bit in range(n_grp.bit_length() - 1):
            if (k >> bit) & 1:
                index = flip(index, bit)
        return index

    def step_bit(h, t):
        return 1 + (h + t) % bits

    def remote(src, dst, send, recv, **device):
        return pltpu.make_async_remote_copy(
            src_ref=src, dst_ref=dst, send_sem=send, recv_sem=recv,
            device_id=device, device_id_type=MESH,
        )

    order = [0, 1, 3, 2] if n_grp >= 4 else [0, 1]
    order = order + list(range(len(order), n_grp))

    def take(i):
        return pltpu.make_async_copy(
            half_integrals.at[0, flip_grp(order[i])], taken.at[i % 2], taken_sem.at[i % 2]
        )

    take(0).start()
    barrier = pltpu.get_barrier_semaphore()
    for bit in range(bits + 1):
        pl.semaphore_signal(
            barrier, inc=1, device_id={"wide": flip(w, bit)}, device_id_type=MESH
        )
    for k in range(1, n_grp):
        pl.semaphore_signal(
            barrier, inc=1, device_id={"grp": flip_grp(k)}, device_id_type=MESH
        )

    owners = [plan[a, b] for a in range(plan.shape[0]) for b in range(plan.shape[1])]
    for last in range(slots - 1, 0, -1):
        for a in range(last):
            low = jnp.minimum(owners[a], owners[a + 1])
            owners[a + 1] = jnp.maximum(owners[a], owners[a + 1])
            owners[a] = low

    tile = 256 if virt % 256 == 0 else virt

    @pl.loop(0, virt // 128)
    def _(c):
        columns = pl.ds(pl.multiple_of(c * 128, 128), 128)
        coeff_t[columns, :] = coeff[:, columns].T

    def transform(i, rows_of):
        if i + 1 < n_grp:
            take(i + 1).start()
        take(i).wait()

        for c in range(n_sub):
            rows_of[order[i] * n_sub + c] = jnp.dot(
                coeff_t[...], taken[i % 2, :, c * pb:(c + 1) * pb],
                preferred_element_type=jnp.float32,
            ).astype(jnp.bfloat16)

    transform(0, mine)
    pl.semaphore_wait(barrier, bits + n_grp)

    sent = []

    def go(copy):
        copy.start()
        sent.append(copy)
        return copy

    middle = lax.rem(lax.div(g + 1, 2), 2) if n_grp >= 4 else 0

    def place(j):
        if n_grp < 4 or j // n_sub % 4 < 2:
            return j
        return j + middle * n_sub * (1 - 2 * (j // n_sub % 2))

    def column_of(j):
        k = j // n_sub
        if n_grp < 4 or k % 4 < 2:
            index = flip_grp(k)
        else:
            index = flip_grp(k) + middle * (flip_grp(k ^ 1) - flip_grp(k))
        return pl.multiple_of(index * (n_sub * pb) + j % n_sub * pb, 128)

    def a2a(k):
        for j in range(k * n_sub, (k + 1) * n_sub):
            yield remote(trans.at[j], mine.at[j], a2a_s.at[j], a2a_r.at[j], grp=flip_grp(k))

    def send(k):
        for copy in a2a(k):
            copy.start()

    def wait_sent(k):
        for copy in a2a(k):
            copy.wait_send()

    def second_sends():
        wait_sent(1)
        if n_grp >= 4:
            pl.when(middle == 1)(lambda: wait_sent(3))
            send(2)
        for k in range(4, n_grp):
            send(k)

    def third_sends():
        wait_sent(2)
        send(3)

    near_in, msg_in, own_in = {}, {}, {}

    def start_near(k):
        at = place(k)
        if k >= n_sub:
            arrived = mine.at[at]
            pltpu.make_async_copy(arrived, arrived, a2a_r.at[at]).wait()
        if n_grp >= 4 and k == 3 * n_sub - 1:
            pl.when(middle == 0)(third_sends)
        near_in[k] = go(remote(
            mine.at[at, pl.ds(sib_half, half)], sib.at[k], sib_s.at[k], sib_r.at[k], wide=flip(w, 0)
        ))
        for h in range(paths):
            peer = flip(w, step_bit(h, 0))
            rows = pl.ds(pl.multiple_of(my_half + h * rb, 16), rb)
            near_in[k, h, 0] = go(remote(
                mine.at[at, rows], near.at[k, h, 0], near_s.at[k, h, 0], near_r.at[k, h, 0], wide=peer
            ))

    def finish_near(k):
        near_in[k].wait_recv()
        for h in range(paths):
            peer = flip(w, step_bit(h, 0))
            near_in[k, h, 1] = go(remote(
                sib.at[k, pl.ds(h * rb, rb)], near.at[k, h, 1],
                near_s.at[k, h, 1], near_r.at[k, h, 1], wide=peer,
            ))

    def same(owner, index):
        return owner == index

    def in_far(owner, h, t):
        inside = [0] + [step_bit(h, u) for u in range(t)]
        there = flip(w, step_bit(h, t))
        ok = None
        for bit in range(bits + 1):
            if bit in inside:
                continue
            agree = lax.rem(lax.div(owner, 1 << bit), 2) == lax.rem(lax.div(there, 1 << bit), 2)
            ok = agree if ok is None else jnp.logical_and(ok, agree)
        return ok

    def pick(k, h, t, r, who, unit):
        rows = 32 if rb % 32 == 0 else 16
        at = pl.multiple_of(r * rows, rows)
        value = mine[place(k), pl.ds(pl.multiple_of(my_half + h * rb + at, 16), rows), :]
        first = flip(w, step_bit(h, 0))
        choices = [
            (flip(w, 0), lambda: sib[k, pl.ds(pl.multiple_of(h * rb + at, 16), rows), :]),
            (first, lambda: near[k, h, 0, pl.ds(at, rows), :]),
            (flip(first, 0), lambda: near[k, h, 1, pl.ds(at, rows), :]),
        ]
        for index, load in choices:
            for owner in who:
                value = lax.select(same(owner, index), load(), value)
        for u in range(1, t):
            for owner in who:
                value = lax.select(
                    in_far(owner, h, u), far[k, h, u - 1, unit, pl.ds(at, rows), :], value
                )
        return value

    def row_loop(body):
        rows = 32 if rb % 32 == 0 else 16

        @pl.loop(0, rb // rows)
        def _(r):
            body(r, pl.multiple_of(r * rows, rows), rows)

    def exchange_far(k, t):
        for h in range(paths):
            if t == 1:
                near_in[k, h, 0].wait_recv()
                near_in[k, h, 1].wait_recv()
            else:
                msg_in[k, h, t - 1].wait_recv()

            def body(r, at, rows):
                for unit in range(slots - 1):
                    who = [0, n_wide - 1] if unit == 0 else [owners[unit]]
                    msg[k, h, t - 1, unit, pl.ds(at, rows), :] = pick(k, h, t, r, who, unit)

            row_loop(body)
            msg_in[k, h, t] = go(remote(
                msg.at[k, h, t - 1], far.at[k, h, t - 1],
                msg_s.at[k, h, t - 1], msg_r.at[k, h, t - 1], wide=flip(w, step_bit(h, t)),
            ))

    def to_sibling(k):
        for h in range(paths):
            msg_in[k, h, bits - 1].wait_recv()

            def body(r, at, rows):
                for s in range(slots):
                    unit = 0 if s in (0, slots - 1) else s
                    who = {0: 0, slots - 1: n_wide - 1}.get(s)
                    who = owners[s] if who is None else who
                    owned[k, s, pl.ds(pl.multiple_of(my_half + h * rb + at, 16), rows), :] = pick(
                        k, h, bits, r, [who], unit
                    )

            row_loop(body)
        part = owned.at[k, :, pl.ds(my_half, half), :]
        own_in[k] = go(remote(part, part, own_s.at[k], own_r.at[k], wide=flip(w, 0)))

    contract = (((1,), (1,)), ((), ()))

    def store_rows(k):
        own_in[k].wait_recv()
        outs.append(pltpu.make_async_copy(
            owned.at[k], owned_out.at[:, :, pl.ds(column_of(k), pb)], owned_sem.at[k]
        ))
        outs[-1].start()

    def term_of(j, s, part):
        straight = lax.dot_general(
            mine[place(j)], owned[j, s, part, :], contract, preferred_element_type=jnp.float32
        )
        turned = lax.dot_general(
            owned[j, s], mine[place(j), part, :], contract, preferred_element_type=jnp.float32
        )
        return 2.0 * straight - turned

    def intersect(parts, lowest, highest):
        @pl.loop(lowest, highest)
        def _(s):
            @pl.loop(0, virt // tile)
            def _(r):
                part = pl.ds(pl.multiple_of(r * tile, tile), tile)
                value = None if parts[0] == 0 else acc[s, :, part]
                for j in parts:
                    term = term_of(j, s, part)
                    value = term if value is None else value + term
                acc[s, :, part] = value

    outs = []
    start_near(0)
    transform(1, trans)
    send(1)
    finish_near(0)
    for i in range(2, n_grp):
        transform(i, trans)
        if order[i] == 3:
            pl.when(middle == 1)(lambda: send(3))

    @pl.loop(0, virt // 128)
    def _(c):
        part = pl.ds(pl.multiple_of(c * 128, 128), 128)
        vir_row[:, part] = vir[part].reshape(1, 128)
        vir_col[part, :] = jnp.broadcast_to(vir[part].reshape(1, 128), (128, 128)).T

    cut = slots // 2
    todo = []
    for j in range(n_parts):
        if j + 1 < n_parts:
            if j + 1 == 2 * n_sub - 1:
                second_sends()
            start_near(j + 1)
            finish_near(j + 1)
        for t in range(1, bits):
            exchange_far(j, t)
        if j:
            to_sibling(j - 1)
        if j >= 2:
            store_rows(j - 2)
            if (j - 1) % n_sub == 0:
                parts = list(range(j - 1 - n_sub, j - 1))
                todo += [(parts, 0, cut), (parts, cut, slots)]
        for _ in range(2 // n_sub):
            if todo:
                intersect(*todo.pop(0))
    for item in todo:
        intersect(*item)
    to_sibling(n_parts - 1)
    if n_parts >= 2:
        store_rows(n_parts - 2)
        if n_sub > 1:
            intersect(list(range(n_parts - n_sub, n_parts - 1)), 0, slots)
        else:
            intersect([n_parts - 2], 0, slots)
    store_rows(n_parts - 1)

    for s in range(slots):
        total = occ[g, w] + occ[g, owners[s]]

        @pl.loop(0, virt // tile)
        def _(r):
            part = pl.ds(pl.multiple_of(r * tile, tile), tile)
            value = acc[s, :, part] + term_of(n_parts - 1, s, part)
            denominator = (total - vir_col[:, :1]) - vir_row[:, part]
            comb[:, pl.ds(pl.multiple_of(s * virt + r * tile, tile), tile)] = (
                value / denominator
            ).astype(jnp.bfloat16)

        part = pl.ds(s * virt, virt)
        outs.append(pltpu.make_async_copy(comb.at[:, part], comb_out.at[:, part], comb_sem.at[s]))
        outs[-1].start()
    for copy in outs:
        copy.wait()
    if n_grp >= 4:
        pl.when(middle == 1)(lambda: wait_sent(2))
        pl.when(middle == 0)(lambda: wait_sent(3))
    for k in range(4, n_grp):
        wait_sent(k)
    for copy in sent:
        copy.wait_send()


def density_kernel(comb, owned, out):
    slots, virt, columns = owned.shape
    out[...] = jnp.dot(
        comb[...], owned[...].reshape(slots * virt, columns), preferred_element_type=jnp.float32
    )


def shards(n_grp, n_wide, half_integrals, coeff_virtual, occ_energy, vir_energy, plan):
    basis, virt = coeff_virtual.shape
    aux = half_integrals.shape[3]
    n_sub = 2 if aux % 512 == 0 else 1
    pb = aux // n_sub
    n_parts = n_grp * n_sub
    slots = plan.size
    bits = n_wide.bit_length() - 2
    paths = bits if virt % (32 * bits) == 0 else 1
    rb = virt // 2 // paths
    bf16, f32 = jnp.bfloat16, jnp.float32
    dma = pltpu.SemaphoreType.DMA
    smem = pl.BlockSpec(memory_space=pltpu.SMEM)
    vmem = pl.BlockSpec(memory_space=pltpu.VMEM)
    hbm = pl.BlockSpec(memory_space=pl.ANY)
    flops = 2 * 2 * slots * virt * virt * aux * n_grp
    comb, owned = pl.pallas_call(
        functools.partial(kernel, n_grp, n_wide, slots, paths, n_sub),
        out_shape=[
            jax.ShapeDtypeStruct((virt, slots * virt), bf16),
            jax.ShapeDtypeStruct((slots, virt, n_grp * aux), bf16),
        ],
        in_specs=[smem, smem, vmem, vmem, hbm],
        out_specs=[hbm, hbm],
        scratch_shapes=[
            pltpu.VMEM((n_parts, virt, pb), bf16),
            pltpu.VMEM((n_parts, virt // 2, pb), bf16),
            pltpu.VMEM((n_parts, paths, 2, rb, pb), bf16),
            pltpu.VMEM((n_parts, paths, bits - 1, slots - 1, rb, pb), bf16),
            pltpu.VMEM((n_parts, paths, bits - 1, slots - 1, rb, pb), bf16),
            pltpu.VMEM((n_parts, slots, virt, pb), bf16),
            pltpu.VMEM((slots, virt, virt), f32),
            pltpu.VMEM((virt, slots * virt), bf16),
            pltpu.VMEM((n_parts, virt, pb), bf16),
            pltpu.VMEM((2, basis, aux), bf16),
            pltpu.VMEM((virt, basis), bf16),
            pltpu.VMEM((virt, 128), f32),
            pltpu.VMEM((1, virt), f32),
            dma((2,)),
            dma((n_parts,)), dma((n_parts,)),
            dma((n_parts,)), dma((n_parts,)),
            dma((n_parts, paths, 2)), dma((n_parts, paths, 2)),
            dma((n_parts, paths, bits - 1)), dma((n_parts, paths, bits - 1)),
            dma((n_parts,)), dma((n_parts,)),
            dma((n_parts,)), dma((slots,)),
        ],
        compiler_params=pltpu.CompilerParams(
            collective_id=0, has_side_effects=True, vmem_limit_bytes=63 * 1024 * 1024
        ),
        cost_estimate=pl.CostEstimate(
            flops=flops, bytes_accessed=16 * virt * aux * n_grp, transcendentals=0
        ),
    )(plan, occ_energy.T, vir_energy, coeff_virtual, half_integrals)
    span = n_grp * aux
    wide_tile = 256 if span % 256 == 0 else span
    density = pl.pallas_call(
        density_kernel,
        out_shape=jax.ShapeDtypeStruct((virt, span), f32),
        grid=(span // wide_tile,),
        in_specs=[
            pl.BlockSpec((virt, slots * virt), lambda c: (0, 0)),
            pl.BlockSpec((slots, virt, wide_tile), lambda c: (0, 0, c)),
        ],
        out_specs=pl.BlockSpec((virt, wide_tile), lambda c: (0, c)),
        compiler_params=pltpu.CompilerParams(vmem_limit_bytes=63 * 1024 * 1024),
        cost_estimate=pl.CostEstimate(
            flops=2 * slots * virt * virt * span, bytes_accessed=14 * virt * span,
            transcendentals=0,
        ),
    )(comb, owned)
    return density[None, None]


def solution(mesh):
    return jax.shard_map(
        functools.partial(shards, mesh.shape["grp"], mesh.shape["wide"]),
        mesh=mesh,
        in_specs=(P("wide", None, None, "grp"), P(), P(), P(), P()),
        out_specs=P("wide", "grp", None, None),
        check_vma=False,
    )
```
